32 devices in a mesh: layer: 2 (over x), rows: 16 (over z, y, core).
Axes of the slice: x: 2, y: 2, z: 4, core: 2. Of those that a mesh axis runs over, the one named last changes fastest.
Arguments:
- down_sources: bfloat16 [2, 32, 16384], P('layer', None, 'rows'), may hold values from -6 to 6
- up_sources: bfloat16 [2, 32, 16384], P('layer', None, 'rows'), may hold values from -6 to 6
- down_tiles: bfloat16 [2, 1024, 128, 128], P('layer', 'rows'), may hold values from -0.1875 to 0.1875
- up_tiles: bfloat16 [2, 1024, 128, 128], P('layer', 'rows'), may hold values from -0.1875 to 0.1875
- tile_rows: int32 [2, 1024], P('layer', 'rows'), may hold values from 0 to 127, as said below
- tile_cols: int32 [2, 1024], P('layer', 'rows'), may hold values from 0 to 127, as said below
- shot_order: int32 [32], replicated, may hold values from 0 to 31, each once
Outputs:
- traces: bfloat16 [2, 32, 16384], P('layer', None, 'rows')
The draws below stay inside these ranges and needn't reach their ends.
Inputs may be any that keep to these rules, and one draw needn't show every extreme that they name: `tile_rows`: in every layer, tile t lies in the tile rows of index t // 64 of the rows axis: 8 * (t // 64) to 8 * (t // 64) + 7. `tile_cols`: every tile's column differs from its row by at most 8. `shot_order`: A permutation of the shots.
All inputs are finite; a program needn't handle non-finite values.
Results may differ from the reference program's by a relative error of at most 0.011.
Values may be sent and summed in bfloat16 or wider, within the bound.
No kernel may reach another device: no remote copies, remote signals or barrier semaphores. Data moves between devices by JAX's collectives and lax.ppermute only.
A program may use at most 64 MiB of HBM per device.

```python
import jax
import jax.numpy as jnp
from jax import lax

M = 16384
TILE = 128
TILES = 1024
SHOTS = 32
TROWS = 128
TR_DEV = 8
TILES_DEV = 64
LAYERS = 2


def tile_layout(key):
    owner = jnp.arange(TILES, dtype=jnp.int32) // TILES_DEV
    within = jax.random.randint(jax.random.fold_in(key, 11), (LAYERS, TILES), 0, TR_DEV, dtype=jnp.int32)
    rows = owner[None, :] * TR_DEV + within
    offset = jax.random.randint(jax.random.fold_in(key, 12), (LAYERS, TILES), -TR_DEV, TR_DEV + 1, dtype=jnp.int32)
    cols = jnp.clip(rows + offset, 0, TROWS - 1)
    return (rows, cols)


def draw_tile_rows(key, part):
    return tile_layout(key)[0]


def draw_tile_cols(key, part):
    return tile_layout(key)[1]


def shard_levels(stream_key, shape, shards, smallest, high):
    def one(axis_at, parts):
        draws = jax.random.uniform(jax.random.fold_in(jax.random.fold_in(stream_key, 6), axis_at), (parts,), jnp.float32, smallest / len(shards), high / len(shards))
        return jnp.repeat(jnp.exp(draws), shape[axis_at] // parts).reshape((-1,) + (1,) * (len(shape) - axis_at - 1))

    level = one(*shards[0])
    for cut in shards[1:]:
        level = level * one(*cut)
    return level


def scatter_about(own_key, extent, width, reach, shards=(), kind=jnp.bfloat16):
    entries = width * jax.random.normal(own_key, extent, jnp.float32)
    if shards:
        entries = entries * shard_levels(own_key, extent, shards, -0.22, 0.18)
    return jnp.clip(entries, -reach, reach).astype(kind)


def setup_inputs(seed: int = 0) -> dict:
    seeds = jax.random.split(jax.random.key(seed), 8)
    down_sources = scatter_about(seeds[0], (LAYERS, SHOTS, M), 1.0, 6.0, ((0, 2), (2, 16)))
    up_sources = scatter_about(seeds[1], (LAYERS, SHOTS, M), 1.0, 6.0, ((0, 2), (2, 16)))
    down_tiles = scatter_about(seeds[2], (LAYERS, TILES, TILE, TILE), (TILE * TILES // TROWS) ** -0.5, 0.1875, ((0, 2), (1, 16)))
    up_tiles = scatter_about(seeds[3], (LAYERS, TILES, TILE, TILE), (TILE * TILES // TROWS) ** -0.5, 0.1875, ((0, 2), (1, 16)))
    tile_rows = draw_tile_rows(jax.random.fold_in(seeds[7], 71), 0)
    tile_cols = draw_tile_cols(jax.random.fold_in(seeds[7], 71), 0)
    shot_order = jax.random.permutation(seeds[6], SHOTS).astype(jnp.int32)
    return {"down_sources": down_sources, "up_sources": up_sources, "down_tiles": down_tiles, "up_tiles": up_tiles, "tile_rows": tile_rows, "tile_cols": tile_cols, "shot_order": shot_order}


def apply_layer(tiles, rows, cols, trace):
    blocks = trace.reshape(SHOTS, TROWS, TILE)
    picked = jnp.take(blocks, cols.astype(jnp.int32), axis=1).astype(jnp.float32)
    product = jnp.einsum('tij,stj->sti', tiles.astype(jnp.float32), picked, precision=lax.Precision.HIGHEST)
    onehot = (rows[:, None] == jnp.arange(TROWS, dtype=jnp.int32)[None, :]).astype(jnp.float32)
    summed = jnp.einsum('sti,tr->sri', product, onehot, precision=lax.Precision.HIGHEST)
    return summed.reshape(SHOTS, M)


def reference(down_sources, up_sources, down_tiles, up_tiles, tile_rows, tile_cols, shot_order):
    order = shot_order.astype(jnp.int32)
    forward = jnp.take(down_sources, order, axis=1)
    backward = jnp.take(up_sources, order, axis=1)
    downs = [forward[0]]
    for layer in range(1, LAYERS):
        term = apply_layer(down_tiles[layer], tile_rows[layer], tile_cols[layer], downs[-1])
        downs.append((forward[layer].astype(jnp.float32) + term).astype(jnp.bfloat16))
    ups = [backward[LAYERS - 1]]
    for layer in range(LAYERS - 2, -1, -1):
        term = apply_layer(up_tiles[layer], tile_rows[layer], tile_cols[layer], ups[-1])
        ups.append((backward[layer].astype(jnp.float32) + term).astype(jnp.bfloat16))
    ups = ups[::-1]
    result = [(downs[k].astype(jnp.float32) + ups[k].astype(jnp.float32)).astype(jnp.bfloat16) for k in range(LAYERS)]
    return jnp.stack(result, axis=0)
```

```python
import functools

import jax
import jax.numpy as jnp
from jax import lax
from jax.experimental import pallas as pl
from jax.experimental.pallas import tpu as pltpu
from jax.sharding import PartitionSpec as P

TILE = 128
VMEM_BYTES = 32 * 1024 * 1024


def wavefront(layers):
    steps = []
    for t in range(layers - 1):
        down, up = (t, t + 1), (layers - 1 - t, layers - 2 - t)
        if down[0] == up[0] or down[1] == up[1]:
            steps += [(down, None), (None, up)]
        else:
            steps.append((down, up))
    return steps


def partner(r, rows):
    other = r ^ 1
    return other if other < rows else r


def farther(r, rows):
    other = r + 1 if r % 2 else r - 1
    return other if 0 <= other < rows else r


def exchange(block, moves, layers, rows):
    moves = [m for m in moves if m is not None]
    axes = ("layer", "rows")
    near = [(s * rows + r, d * rows + r) for s, d in moves for r in range(rows)]
    far = [(s * rows + r, d * rows + farther(r, rows)) for s, d in moves for r in range(rows)]
    inner = [(r, partner(r, rows)) for r in range(rows)]
    own = lax.ppermute(block, axes, near)
    distant = lax.ppermute(block, axes, far)
    beside = lax.ppermute(own, "rows", inner)
    return own, beside, distant


def pick_kernel(up_layer, down_tiles, up_tiles, picked, sem):
    upward = lax.axis_index("layer") == up_layer

    @pl.when(upward)
    def _():
        pltpu.make_async_copy(up_tiles.at[0], picked, sem).start()

    @pl.when(jnp.logical_not(upward))
    def _():
        pltpu.make_async_copy(down_tiles.at[0], picked, sem).start()

    pltpu.make_async_copy(down_tiles.at[0], picked, sem).wait()


def pick_tiles(down_tiles, up_tiles, up_layer):
    tiles = down_tiles.shape[1]
    size = down_tiles.size * down_tiles.dtype.itemsize
    return pl.pallas_call(
        functools.partial(pick_kernel, up_layer),
        out_shape=jax.ShapeDtypeStruct((tiles, TILE, TILE), down_tiles.dtype),
        in_specs=[pl.BlockSpec(memory_space=pltpu.HBM)] * 2,
        out_specs=pl.BlockSpec(memory_space=pltpu.VMEM),
        scratch_shapes=[pltpu.SemaphoreType.DMA],
        compiler_params=pltpu.CompilerParams(vmem_limit_bytes=VMEM_BYTES),
        cost_estimate=pl.CostEstimate(flops=0, bytes_accessed=2 * size, transcendentals=0),
        name="pick_tiles",
    )(down_tiles, up_tiles)


def apply_kernel(
    up_layer, down_layer, final,
    tile_rows, tile_cols, order, own, beside, distant, tiles, down, up, out, blocks, total,
):
    count = blocks.shape[0] // 3
    me = lax.axis_index("rows")
    layer = lax.axis_index("layer")
    for place, part in enumerate((own, beside, distant)):
        for k in range(count):
            blocks[place * count + k] = part[0, :, k * TILE:(k + 1) * TILE]
    total[...] = jnp.zeros_like(total)

    def one_tile(t, carry):
        row = tile_rows[0, t] - me * count
        col = tile_cols[0, t]
        index = col // count
        place = jnp.where(index == me, 0, jnp.where(index == (me ^ 1), 1, 2))
        seen = blocks[place * count + col - index * count]
        total[row] += lax.dot_general(
            tiles[t], seen, (((1,), (1,)), ((), ())), preferred_element_type=jnp.float32
        )
        return carry

    lax.fori_loop(0, tiles.shape[0], one_tile, 0, unroll=True)

    upward = layer == up_layer
    active = jnp.logical_or(upward, layer == down_layer)
    shots = own.shape[1]
    if final:
        slots = lax.broadcasted_iota(jnp.int32, (shots, shots), 0)
        onehot = (slots == order[...]).astype(jnp.float32).T.astype(jnp.bfloat16)
    for k in range(count):
        here = slice(k * TILE, (k + 1) * TILE)
        term = jnp.where(active, total[k].T, 0.0)
        below = down[0, :, here].astype(jnp.float32)
        above = up[0, :, here].astype(jnp.float32)
        base = jnp.where(upward, above, below)
        fresh = (base + term).astype(jnp.bfloat16)
        if final:
            rest = jnp.where(upward, below, above)
            both = (fresh.astype(jnp.float32) + rest).astype(jnp.bfloat16)
            fresh = jnp.dot(onehot, both, preferred_element_type=jnp.float32).astype(jnp.bfloat16)
        out[0, :, here] = fresh


def apply_step(tile_rows, tile_cols, order, parts, tiles, down, up, moves, final):
    _, shots, width = down.shape
    count = width // TILE
    down_move, up_move = moves
    vmem = pl.BlockSpec(memory_space=pltpu.VMEM)
    smem = pl.BlockSpec(memory_space=pltpu.SMEM)
    kernel = functools.partial(
        apply_kernel, up_move[1] if up_move else -1, down_move[1] if down_move else -1, final
    )
    return pl.pallas_call(
        kernel,
        out_shape=jax.ShapeDtypeStruct(down.shape, down.dtype),
        in_specs=[smem, smem] + [vmem] * 7,
        out_specs=vmem,
        scratch_shapes=[
            pltpu.VMEM((3 * count, shots, TILE), jnp.bfloat16),
            pltpu.VMEM((count, TILE, shots), jnp.float32),
        ],
        compiler_params=pltpu.CompilerParams(vmem_limit_bytes=VMEM_BYTES),
        cost_estimate=pl.CostEstimate(
            flops=2 * tiles.size * shots, bytes_accessed=tiles.size * 2, transcendentals=0
        ),
        name="apply_step",
    )(tile_rows, tile_cols, order, *parts, tiles, down, up)


def shards(down_sources, up_sources, down_tiles, up_tiles, tile_rows, tile_cols, shot_order):
    layers, rows = lax.axis_size("layer"), lax.axis_size("rows")
    layer = lax.axis_index("layer")
    order = shot_order.reshape(1, -1)
    steps = wavefront(layers)
    down, up = down_sources, up_sources
    for at, moves in enumerate(steps):
        down_move, up_move = moves
        final = at == len(steps) - 1
        if up_move is None:
            leaving = down
        elif down_move is None:
            leaving = up
        else:
            leaving = jnp.where(layer == up_move[0], up, down)
        parts = exchange(leaving, moves, layers, rows)
        tiles = pick_tiles(down_tiles, up_tiles, up_move[1] if up_move else -1)
        fresh = apply_step(tile_rows, tile_cols, order, parts, tiles, down, up, moves, final)
        if final:
            return fresh
        upward = layer == (up_move[1] if up_move else -1)
        down, up = jnp.where(upward, down, fresh), jnp.where(upward, fresh, up)


def solution(mesh):
    return jax.shard_map(
        shards,
        mesh=mesh,
        in_specs=(
            P("layer", None, "rows"),
            P("layer", None, "rows"),
            P("layer", "rows", None, None),
            P("layer", "rows", None, None),
            P("layer", "rows"),
            P("layer", "rows"),
            P(),
        ),
        out_specs=P("layer", None, "rows"),
        check_vma=False,
    )
```

```python
import functools

import jax
import jax.numpy as jnp
from jax import lax
from jax.experimental import pallas as pl
from jax.experimental.pallas import tpu as pltpu
from jax.sharding import PartitionSpec as P

TILE = 128
VMEM_BYTES = 32 * 1024 * 1024


def wavefront(layers):
    steps = []
    for t in range(layers - 1):
        down, up = (t, t + 1), (layers - 1 - t, layers - 2 - t)
        if down[0] == up[0] or down[1] == up[1]:
            steps += [(down, None), (None, up)]
        else:
            steps.append((down, up))
    return steps


def partner(r, rows):
    other = r ^ 1
    return other if other < rows else r


def farther(r, rows):
    other = r + 1 if r % 2 else r - 1
    return other if 0 <= other < rows else r


def exchange(block, moves, layers, rows):
    moves = [m for m in moves if m is not None]
    axes = ("layer", "rows")
    near = [(s * rows + r, d * rows + r) for s, d in moves for r in range(rows)]
    far = [(s * rows + r, d * rows + farther(r, rows)) for s, d in moves for r in range(rows)]
    return lax.ppermute(block, axes, near), lax.ppermute(block, axes, far)


def beside_pairs(rows):
    return [(r, partner(r, rows)) for r in range(rows)]


def prepare_kernel(
    moves, final, down_tiles, up_tiles, tile_rows, tile_cols, order, down, up,
    tiles, lists, shuffle, base, rest, rows_here, cols_here, order_here, down_here, up_here, sems,
):
    count, shots = base.shape[0], base.shape[1]
    layer, me = lax.axis_index("layer"), lax.axis_index("rows")
    down_move, up_move = moves
    upward = layer == up_move[1] if up_move else layer < 0
    active = jnp.logical_or(upward, layer == down_move[1]) if down_move else upward

    small = [
        pltpu.make_async_copy(source, here, sems.at[1 + k])
        for k, (source, here) in enumerate((
            (tile_rows, rows_here), (tile_cols, cols_here), (order, order_here), (down, down_here), (up, up_here)
        ))
    ]
    for copy in small:
        copy.start()

    @pl.when(upward)
    def _():
        pltpu.make_async_copy(up_tiles.at[0], tiles, sems.at[0]).start()

    @pl.when(jnp.logical_not(upward))
    def _():
        pltpu.make_async_copy(down_tiles.at[0], tiles, sems.at[0]).start()

    for copy in small:
        copy.wait()

    n = tile_rows.shape[1]
    pairs = lists.shape[1]
    shift = (3 * count).bit_length()
    even = me % 2 == 0
    row = rows_here[...] - me * count
    seen = cols_here[...] - (me - 1) * count
    before = seen + jnp.where(even, 2 * count, count)
    after = seen - 2 * count + jnp.where(even, count, 2 * count)
    block = jnp.where(seen < count, before, jnp.where(seen < 2 * count, seen - count, after))
    block = jnp.where(active, block, 3 * count)

    def both_ways(value):
        across = jnp.broadcast_to(value.astype(jnp.float32), (n, n))
        return across, across.T

    row_l, row_s = both_ways(row)
    block_s = both_ways(block)[1][:, :1]
    t_l = lax.broadcasted_iota(jnp.int32, (n, n), 1)
    t_s = lax.broadcasted_iota(jnp.int32, (n, n), 0)
    same = row_l == row_s
    rank_l = jnp.sum(jnp.where(same & (t_s < t_l), 1.0, 0.0), axis=0, keepdims=True)
    rank_s = jnp.sum(jnp.where(same & (t_l < t_s), 1.0, 0.0), axis=1, keepdims=True)
    half_l, half_s = jnp.floor(rank_l * 0.5), jnp.floor(rank_s * 0.5)
    first_l, first_s = rank_l == 2.0 * half_l, rank_s == 2.0 * half_s
    ahead = jnp.sum(jnp.where((row_l < row_s) & first_l, 1.0, 0.0), axis=1, keepdims=True)
    place = ahead + half_s
    hit = place == lax.broadcasted_iota(jnp.int32, (n, pairs), 1).astype(jnp.float32)
    hit_a, hit_b = hit & first_s, hit & jnp.logical_not(first_s)

    def listed(hits, value):
        return jnp.sum(jnp.where(hits, value, 0.0), axis=0, keepdims=True)

    number = t_s[:, :1].astype(jnp.float32)
    nothing = 3.0 * count
    block_a = listed(hit_a, block_s - nothing) + nothing
    block_b = listed(hit_b, block_s - nothing) + nothing
    word = (listed(hit_a, row_s[:, :1]) * 2**shift + block_a) * 2**shift + block_b
    lists[0:1, :] = listed(hit_a, number).astype(jnp.int32)
    lists[1:2, :] = listed(hit_b, number).astype(jnp.int32)
    lists[2:3, :] = word.astype(jnp.int32)

    slots = lax.broadcasted_iota(jnp.int32, (shots, shots), 0)
    wanted = order_here[...] if final else lax.broadcasted_iota(jnp.int32, (shots, shots), 1)
    shuffle[...] = (slots == wanted).astype(jnp.float32).T.astype(jnp.bfloat16)
    for k in range(count):
        here = slice(k * TILE, (k + 1) * TILE)
        below, above = down_here[0, :, here], up_here[0, :, here]
        base[k] = jnp.where(upward, above, below).astype(jnp.float32)
        rest[k] = jnp.where(upward, below, above)
    pltpu.make_async_copy(down_tiles.at[0], tiles, sems.at[0]).wait()


def prepare(moves, final, down_tiles, up_tiles, tile_rows, tile_cols, order, down, up):
    tiles = down_tiles.shape[1]
    _, shots, width = down.shape
    count = width // TILE
    pairs = (tiles + min(tiles, count)) // 2
    vmem = pl.BlockSpec(memory_space=pltpu.VMEM)
    size = down_tiles.size * down_tiles.dtype.itemsize
    return pl.pallas_call(
        functools.partial(prepare_kernel, moves, final),
        out_shape=(
            jax.ShapeDtypeStruct((tiles, TILE, TILE), down_tiles.dtype),
            jax.ShapeDtypeStruct((3, pairs), jnp.int32),
            jax.ShapeDtypeStruct((shots, shots), jnp.bfloat16),
            jax.ShapeDtypeStruct((count, shots, TILE), jnp.float32),
            jax.ShapeDtypeStruct((count, shots, TILE), jnp.bfloat16),
        ),
        in_specs=[pl.BlockSpec(memory_space=pl.ANY)] * 7,
        out_specs=(vmem,) * 5,
        scratch_shapes=[
            pltpu.VMEM(value.shape, value.dtype) for value in (tile_rows, tile_cols, order, down, up)
        ] + [pltpu.SemaphoreType.DMA((6,))],
        compiler_params=pltpu.CompilerParams(vmem_limit_bytes=VMEM_BYTES),
        cost_estimate=pl.CostEstimate(flops=0, bytes_accessed=2 * size, transcendentals=0),
        name="prepare",
    )(*(
        pltpu.with_memory_space_constraint(value, pltpu.HBM)
        for value in (down_tiles, up_tiles, tile_rows, tile_cols, order, down, up)
    ))


def arrange_kernel(lists, tiles, weights):
    rows = lax.broadcasted_iota(jnp.int32, (TILE, TILE), 0)
    identity = (rows == lax.broadcasted_iota(jnp.int32, (TILE, TILE), 1)).astype(jnp.bfloat16)
    for p in range(weights.shape[0]):
        weights[p, :TILE] = tiles[lists[0, p]].T
        weights[p, TILE:] = lax.dot_general(
            identity, tiles[lists[1, p]], (((1,), (1,)), ((), ())), preferred_element_type=jnp.float32
        ).astype(jnp.bfloat16)


def arrange(lists, tiles):
    vmem = pl.BlockSpec(memory_space=pltpu.VMEM)
    pairs = lists.shape[1]
    return pl.pallas_call(
        arrange_kernel,
        out_shape=jax.ShapeDtypeStruct((pairs, 2 * TILE, TILE), tiles.dtype),
        in_specs=[vmem] * 2,
        out_specs=vmem,
        compiler_params=pltpu.CompilerParams(vmem_limit_bytes=VMEM_BYTES),
        cost_estimate=pl.CostEstimate(flops=0, bytes_accessed=2 * tiles.size * 2, transcendentals=0),
        name="arrange",
    )(lists, tiles)


def apply_kernel(lists, shuffle, own, beside, distant, weights, base, rest, out, blocks, total):
    count, shots = base.shape[0], base.shape[1]
    shift = (3 * count).bit_length()
    for place, part in enumerate((own, beside, distant)):
        for k in range(count):
            blocks[place * count + k] = part[0, :, k * TILE:(k + 1) * TILE]
    blocks[3 * count] = jnp.zeros((shots, TILE), jnp.bfloat16)
    total[...] = base[...]
    mask = 2**shift - 1
    for p in range(weights.shape[0]):
        word = lists[2, p]
        read = jnp.concatenate([blocks[(word >> shift) & mask], blocks[word & mask]], axis=1)
        total[word >> (2 * shift)] += jnp.dot(read, weights[p], preferred_element_type=jnp.float32)
    for k in range(count):
        fresh = total[k].astype(jnp.bfloat16)
        if rest is not None:
            fresh = (fresh.astype(jnp.float32) + rest[k].astype(jnp.float32)).astype(jnp.bfloat16)
        fresh = jnp.dot(shuffle[...], fresh, preferred_element_type=jnp.float32)
        out[0, :, k * TILE:(k + 1) * TILE] = fresh.astype(jnp.bfloat16)


def apply_step(lists, shuffle, parts, weights, base, rest, final):
    count, shots, _ = base.shape
    vmem = pl.BlockSpec(memory_space=pltpu.VMEM)

    def kernel(lists, shuffle, own, beside, distant, weights, base, rest, *others):
        apply_kernel(
            lists, shuffle, own, beside, distant, weights, base, rest if final else None, *others
        )

    return pl.pallas_call(
        kernel,
        out_shape=jax.ShapeDtypeStruct((1, shots, count * TILE), jnp.bfloat16),
        in_specs=[vmem] * 8,
        out_specs=vmem,
        scratch_shapes=[
            pltpu.VMEM((3 * count + 1, shots, TILE), jnp.bfloat16),
            pltpu.VMEM((count, shots, TILE), jnp.float32),
        ],
        compiler_params=pltpu.CompilerParams(vmem_limit_bytes=VMEM_BYTES),
        cost_estimate=pl.CostEstimate(
            flops=2 * weights.size * shots, bytes_accessed=weights.size * 2, transcendentals=0
        ),
        name="apply_step",
    )(lists, shuffle, *parts, weights, base, rest)


def shards(down_sources, up_sources, down_tiles, up_tiles, tile_rows, tile_cols, shot_order):
    layers, rows = lax.axis_size("layer"), lax.axis_size("rows")
    layer = lax.axis_index("layer")
    order = shot_order.reshape(1, -1)
    steps = wavefront(layers)
    down, up = down_sources, up_sources
    for at, moves in enumerate(steps):
        down_move, up_move = moves
        final = at == len(steps) - 1
        if up_move is None:
            leaving = down
        elif down_move is None:
            leaving = up
        else:
            leaving = jnp.where(layer == up_move[0], up, down)
        own, distant = exchange(leaving, moves, layers, rows)
        tiles, lists, shuffle, base, rest = prepare(
            moves, final, down_tiles, up_tiles, tile_rows, tile_cols, order, down, up
        )
        own, lists = lax.optimization_barrier((own, lists))
        parts = own, lax.ppermute(own, "rows", beside_pairs(rows)), distant
        fresh = apply_step(lists, shuffle, parts, arrange(lists, tiles), base, rest, final)
        if final:
            return fresh
        upward = layer == (up_move[1] if up_move else -1)
        down, up = jnp.where(upward, down, fresh), jnp.where(upward, fresh, up)


def solution(mesh):
    return jax.shard_map(
        shards,
        mesh=mesh,
        in_specs=(
            P("layer", None, "rows"),
            P("layer", None, "rows"),
            P("layer", "rows", None, None),
            P("layer", "rows", None, None),
            P("layer", "rows"),
            P("layer", "rows"),
            P(),
        ),
        out_specs=P("layer", None, "rows"),
        check_vma=False,
    )
```

```python
import functools

import jax
import jax.numpy as jnp
from jax import lax
from jax.experimental import pallas as pl
from jax.experimental.pallas import tpu as pltpu
from jax.sharding import PartitionSpec as P

TILE = 128
VMEM_BYTES = 32 * 1024 * 1024


def wavefront(layers):
    steps = []
    for t in range(layers - 1):
        down, up = (t, t + 1), (layers - 1 - t, layers - 2 - t)
        if down[0] == up[0] or down[1] == up[1]:
            steps += [(down, None), (None, up)]
        else:
            steps.append((down, up))
    return steps


def partner(r, rows):
    other = r ^ 1
    return other if other < rows else r


def farther(r, rows):
    other = r + 1 if r % 2 else r - 1
    return other if 0 <= other < rows else r


def across(block, moves, rows):
    moves = [m for m in moves if m is not None]
    axes = ("layer", "rows")
    near = [(s * rows + r, d * rows + partner(r, rows)) for s, d in moves for r in range(rows)]
    far = [(s * rows + r, d * rows + farther(r, rows)) for s, d in moves for r in range(rows)]
    return lax.ppermute(block, axes, near), lax.ppermute(duplicate(block), axes, far)


def duplicate(block):
    def kernel(block, out):
        out[...] = block[...]

    return call(kernel, "duplicate", block, flops=3 * 10**9)(block)


def call(kernel, name, out, scratch=(), flops=0, moved=0):
    vmem = pl.BlockSpec(memory_space=pltpu.VMEM)
    shapes = jax.tree.map(lambda leaf: jax.ShapeDtypeStruct(leaf.shape, leaf.dtype), out)

    def run(*operands):
        return pl.pallas_call(
            kernel,
            out_shape=shapes,
            in_specs=[vmem] * len(operands),
            out_specs=jax.tree.map(lambda _: vmem, shapes),
            scratch_shapes=scratch,
            compiler_params=pltpu.CompilerParams(vmem_limit_bytes=VMEM_BYTES),
            cost_estimate=pl.CostEstimate(flops=flops, bytes_accessed=moved, transcendentals=0),
            name=name,
        )(*operands)

    return run


def roles(moves):
    layer = lax.axis_index("layer")
    down_move, up_move = moves
    upward = layer == (up_move[1] if up_move else -1)
    downward = layer == (down_move[1] if down_move else -1)
    return upward, jnp.logical_or(upward, downward)


def bits(tiles, count):
    return (2 * count).bit_length(), (tiles - 1).bit_length()


def prepare_kernel(moves, final, count, tile_rows, tile_cols, order, lists, shuffle):
    _, active = roles(moves)
    me = lax.axis_index("rows")
    n, shots = tile_rows.shape[1], shuffle.shape[0]
    pairs = lists.shape[1]
    block_bits, tile_bits = bits(n, count)
    even = me % 2 == 0
    row = tile_rows[...] - me * count
    seen = tile_cols[...] - (me - 1) * count
    far_start, beside_start = jnp.where(even, 0, 2 * count), jnp.where(even, 2 * count, 0)
    far = (seen >= far_start) & (seen < far_start + count)
    mine = (seen >= count) & (seen < 2 * count)
    near = jnp.where(mine, seen - count, seen - beside_start + count)
    block = jnp.where(far, seen - far_start, near)
    block = jnp.where(active, block, 2 * count)
    line = row + jnp.where(far, count, 0)

    def both_ways(value):
        wide = jnp.broadcast_to(value.astype(jnp.float32), (n, n))
        return wide, wide.T

    line_l, line_s = both_ways(line)
    block_s = both_ways(block)[1][:, :1]
    t_l = lax.broadcasted_iota(jnp.int32, (n, n), 1)
    t_s = lax.broadcasted_iota(jnp.int32, (n, n), 0)
    same = line_l == line_s
    rank_l = jnp.sum(jnp.where(same & (t_s < t_l), 1.0, 0.0), axis=0, keepdims=True)
    rank_s = jnp.sum(jnp.where(same & (t_l < t_s), 1.0, 0.0), axis=1, keepdims=True)
    half_l, half_s = jnp.floor(rank_l * 0.5), jnp.floor(rank_s * 0.5)
    first_l, first_s = rank_l == 2.0 * half_l, rank_s == 2.0 * half_s
    number = t_s[:, :1].astype(jnp.float32)
    code_s = number * 2**block_bits + block_s
    nothing = 2.0 * count
    slot = lax.broadcasted_iota(jnp.int32, (n, pairs), 1).astype(jnp.float32)

    def listed(hits, value):
        return jnp.sum(jnp.where(hits, value, 0.0), axis=0, keepdims=True)

    for group in range(2):
        low, high = group * count, (group + 1) * count
        member = (line_s[:, :1] >= low) & (line_s[:, :1] < high)
        counted = (line_l >= low) & (line_l < line_s) & first_l
        ahead = jnp.sum(jnp.where(counted, 1.0, 0.0), axis=1, keepdims=True)
        hit = (ahead + half_s == slot) & member
        hit_a, hit_b = hit & first_s, hit & jnp.logical_not(first_s)
        here = (line_s[:, :1] - low) * 2 ** (block_bits + tile_bits)
        word_a = listed(hit_a, here + code_s - nothing) + nothing
        word_b = listed(hit_b, code_s - nothing) + nothing
        lists[2 * group : 2 * group + 1, :] = word_a.astype(jnp.int32)
        lists[2 * group + 1 : 2 * group + 2, :] = word_b.astype(jnp.int32)
        used = jnp.sum(listed(hit_a, jnp.ones_like(number)), axis=1, keepdims=True)
    lists[4:5, :] = jnp.broadcast_to(used.astype(jnp.int32), (1, pairs))

    slots = lax.broadcasted_iota(jnp.int32, (shots, shots), 0)
    wanted = order[...] if final else lax.broadcasted_iota(jnp.int32, (shots, shots), 1)
    shuffle[...] = (slots == wanted).astype(jnp.float32).T.astype(jnp.bfloat16)


def arrange_kernel(moves, down_tiles, up_tiles, weights):
    rows = lax.broadcasted_iota(jnp.int32, (TILE, TILE), 0)
    identity = (rows == lax.broadcasted_iota(jnp.int32, (TILE, TILE), 1)).astype(jnp.bfloat16)
    upward, _ = roles(moves)

    def lay(tiles):
        for t in range(weights.shape[0]):
            if t % 2:
                weights[t] = lax.dot_general(
                    identity, tiles[0, t], (((1,), (1,)), ((), ())), preferred_element_type=jnp.float32
                ).astype(jnp.bfloat16)
            else:
                weights[t] = tiles[0, t].T

    pl.when(upward)(lambda: lay(up_tiles))
    pl.when(jnp.logical_not(upward))(lambda: lay(down_tiles))


def add_products(lists, group, pairs, blocks, weights, total):
    block_bits, tile_bits = bits(weights.shape[0], total.shape[0])
    block_mask, tile_mask = 2**block_bits - 1, 2**tile_bits - 1
    for p in range(*pairs):
        a, b = lists[2 * group, p], lists[2 * group + 1, p]
        read = jnp.concatenate([blocks[a & block_mask], blocks[b & block_mask]], axis=1)
        tile_a, tile_b = (a >> block_bits) & tile_mask, b >> block_bits
        both = jnp.concatenate([weights[tile_a], weights[tile_b]], axis=0)
        row = a >> (block_bits + tile_bits)
        total[row] += jnp.dot(read, both, preferred_element_type=jnp.float32)


def near_kernel(moves, lists, own, beside, weights, down, up, total, blocks):
    count, shots = total.shape[0], total.shape[1]
    upward, _ = roles(moves)
    for k in range(count):
        here = slice(k * TILE, (k + 1) * TILE)
        blocks[k] = own[0, :, here]
        blocks[count + k] = beside[0, :, here]
        total[k] = jnp.where(upward, up[0, :, here], down[0, :, here]).astype(jnp.float32)
    blocks[2 * count] = jnp.zeros((shots, TILE), jnp.bfloat16)
    add_products(lists, 0, (0, lists.shape[1]), blocks, weights, total)


def far_kernel(moves, final, lists, shuffle, distant, weights, near_total, down, up, out, blocks, total):
    count, shots = total.shape[0], total.shape[1]
    upward, _ = roles(moves)
    for k in range(count):
        blocks[k] = distant[0, :, k * TILE:(k + 1) * TILE]
    blocks[2 * count] = jnp.zeros((shots, TILE), jnp.bfloat16)
    total[...] = near_total[...]
    pairs = lists.shape[1]
    usual, most = -(-pairs // 3), -(-4 * pairs // 9)
    used = lists[4, 0]
    add_products(lists, 1, (0, usual), blocks, weights, total)
    pl.when(used > usual)(lambda: add_products(lists, 1, (usual, most), blocks, weights, total))
    pl.when(used > most)(lambda: add_products(lists, 1, (most, pairs), blocks, weights, total))
    for k in range(count):
        here = slice(k * TILE, (k + 1) * TILE)
        fresh = total[k].astype(jnp.bfloat16)
        if final:
            rest = jnp.where(upward, down[0, :, here], up[0, :, here])
            fresh = (fresh.astype(jnp.float32) + rest.astype(jnp.float32)).astype(jnp.bfloat16)
        fresh = jnp.dot(shuffle[...], fresh, preferred_element_type=jnp.float32)
        out[0, :, here] = fresh.astype(jnp.bfloat16)


def step(moves, final, leaving, down, up, down_tiles, up_tiles, tile_rows, tile_cols, order):
    rows = lax.axis_size("rows")
    _, shots, width = down.shape
    tiles, count = tile_rows.shape[1], width // TILE
    pairs = (tiles + min(tiles, count)) // 2
    shape = jax.ShapeDtypeStruct
    sums = shape((count, shots, TILE), jnp.float32)
    blocks = pltpu.VMEM((2 * count + 1, shots, TILE), jnp.bfloat16)

    beside, distant = across(leaving, moves, rows)
    lists, shuffle = call(
        functools.partial(prepare_kernel, moves, final, count),
        "prepare",
        (shape((5, pairs), jnp.int32), shape((shots, shots), jnp.bfloat16)),
    )(tile_rows, tile_cols, order)
    beside, lists = lax.optimization_barrier((beside, lists))
    own = lax.ppermute(beside, "rows", [(r, partner(r, rows)) for r in range(rows)])
    weights = call(
        functools.partial(arrange_kernel, moves),
        "arrange",
        shape((tiles, TILE, TILE), down_tiles.dtype),
        flops=3 * 10**9,
    )(down_tiles, up_tiles)
    total = call(functools.partial(near_kernel, moves), "near", sums, [blocks])(
        lists, own, beside, weights, down, up
    )
    return call(
        functools.partial(far_kernel, moves, final),
        "far",
        down,
        [blocks, pltpu.VMEM(sums.shape, sums.dtype)],
    )(lists, shuffle, distant, weights, total, down, up)


def shards(down_sources, up_sources, down_tiles, up_tiles, tile_rows, tile_cols, shot_order):
    layer = lax.axis_index("layer")
    order = shot_order.reshape(1, -1)
    steps = wavefront(lax.axis_size("layer"))
    down, up = down_sources, up_sources
    for at, moves in enumerate(steps):
        down_move, up_move = moves
        if up_move is None:
            leaving = down
        elif down_move is None:
            leaving = up
        else:
            leaving = jnp.where(layer == up_move[0], up, down)
        final = at == len(steps) - 1
        fresh = step(
            moves, final, leaving, down, up, down_tiles, up_tiles, tile_rows, tile_cols, order
        )
        if final:
            return fresh
        upward, _ = roles(moves)
        down, up = jnp.where(upward, down, fresh), jnp.where(upward, fresh, up)


def solution(mesh):
    return jax.shard_map(
        shards,
        mesh=mesh,
        in_specs=(
            P("layer", None, "rows"),
            P("layer", None, "rows"),
            P("layer", "rows", None, None),
            P("layer", "rows", None, None),
            P("layer", "rows"),
            P("layer", "rows"),
            P(),
        ),
        out_specs=P("layer", None, "rows"),
        check_vma=False,
    )
```

```python
import functools

import jax
import jax.numpy as jnp
from jax import lax
from jax.experimental import pallas as pl
from jax.experimental.pallas import tpu as pltpu
from jax.sharding import PartitionSpec as P

TILE = 128
VMEM_BYTES = 32 * 1024 * 1024


def wavefront(layers):
    steps = []
    for t in range(layers - 1):
        down, up = (t, t + 1), (layers - 1 - t, layers - 2 - t)
        if down[0] == up[0] or down[1] == up[1]:
            steps += [(down, None), (None, up)]
        else:
            steps.append((down, up))
    return steps


def partner(r, rows):
    other = r ^ 1
    return other if other < rows else r


def farther(r, rows):
    other = r + 1 if r % 2 else r - 1
    return other if 0 <= other < rows else r


def crosses(r):
    return r < 2


def across(block, moves, rows):
    moves = [m for m in moves if m is not None]
    axes = ("layer", "rows")
    first = [partner(r, rows) if crosses(r) else r for r in range(rows)]
    near = [(s * rows + r, d * rows + first[r]) for s, d in moves for r in range(rows)]
    far = [(s * rows + r, d * rows + farther(r, rows)) for s, d in moves for r in range(rows)]
    return lax.ppermute(block, axes, near), lax.ppermute(duplicate(block), axes, far)


def duplicate(block):
    def kernel(block, out):
        out[...] = block[...]

    return call(kernel, "duplicate", block, flops=3 * 10**9)(block)


def call(kernel, name, out, scratch=(), flops=0):
    vmem = pl.BlockSpec(memory_space=pltpu.VMEM)
    shapes = jax.tree.map(lambda leaf: jax.ShapeDtypeStruct(leaf.shape, leaf.dtype), out)

    def run(*operands):
        return pl.pallas_call(
            kernel,
            out_shape=shapes,
            in_specs=[vmem] * len(operands),
            out_specs=jax.tree.map(lambda _: vmem, shapes),
            scratch_shapes=scratch,
            compiler_params=pltpu.CompilerParams(vmem_limit_bytes=VMEM_BYTES),
            cost_estimate=pl.CostEstimate(flops=flops, bytes_accessed=0, transcendentals=0),
            name=name,
        )(*operands)

    return run


def roles(moves):
    layer = lax.axis_index("layer")
    down_move, up_move = moves
    upward = layer == (up_move[1] if up_move else -1)
    downward = layer == (down_move[1] if down_move else -1)
    return upward, jnp.logical_or(upward, downward)


def bits(tiles, count):
    return count.bit_length(), (tiles - 1).bit_length()


def prepare_kernel(
    moves, count, tile_rows, tile_cols, order, down_tiles, up_tiles, lists, source, weights
):
    arrange(moves, down_tiles, up_tiles, weights)
    _, active = roles(moves)
    me = lax.axis_index("rows")
    n, shots = tile_rows.shape[1], source.shape[0]
    pairs = lists.shape[1]
    column_bits, tile_bits = bits(n, count)
    even = me % 2 == 0
    row = tile_rows[...] - me * count
    seen = tile_cols[...] - (me - 1) * count
    far_start, beside_start = jnp.where(even, 0, 2 * count), jnp.where(even, 2 * count, 0)
    first_start = jnp.where(crosses(me), beside_start, count)
    far = (seen >= far_start) & (seen < far_start + count)
    first = (seen >= first_start) & (seen < first_start + count)
    group = jnp.where(far, 2, jnp.where(first, 0, 1))
    column = seen - jnp.where(seen < count, 0, jnp.where(seen < 2 * count, count, 2 * count))
    column = jnp.where(active, column, count)
    line = row + group * count

    def both_ways(value):
        wide = jnp.broadcast_to(value.astype(jnp.float32), (n, n))
        return wide, wide.T

    line_l, line_s = both_ways(line)
    column_s = both_ways(column)[1][:, :1]
    t_l = lax.broadcasted_iota(jnp.int32, (n, n), 1)
    t_s = lax.broadcasted_iota(jnp.int32, (n, n), 0)
    same = line_l == line_s
    rank_l = jnp.sum(jnp.where(same & (t_s < t_l), 1.0, 0.0), axis=0, keepdims=True)
    rank_s = jnp.sum(jnp.where(same & (t_l < t_s), 1.0, 0.0), axis=1, keepdims=True)
    half_l, half_s = jnp.floor(rank_l * 0.5), jnp.floor(rank_s * 0.5)
    first_l, first_s = rank_l == 2.0 * half_l, rank_s == 2.0 * half_s
    number = t_s[:, :1].astype(jnp.float32)
    code_s = number * 2**column_bits + column_s
    nothing = float(count)
    slot = lax.broadcasted_iota(jnp.int32, (n, pairs), 1).astype(jnp.float32)

    def listed(hits, value):
        return jnp.sum(jnp.where(hits, value, 0.0), axis=0, keepdims=True)

    for group in range(3):
        low, high = group * count, (group + 1) * count
        member = (line_s[:, :1] >= low) & (line_s[:, :1] < high)
        counted = (line_l >= low) & (line_l < line_s) & first_l
        ahead = jnp.sum(jnp.where(counted, 1.0, 0.0), axis=1, keepdims=True)
        hit = (ahead + half_s == slot) & member
        hit_a, hit_b = hit & first_s, hit & jnp.logical_not(first_s)
        here = (line_s[:, :1] - low) * 2 ** (column_bits + tile_bits)
        word_a = listed(hit_a, here + code_s - nothing) + nothing
        word_b = listed(hit_b, code_s - nothing) + nothing
        used = jnp.sum(listed(hit_a, jnp.ones_like(number)), axis=1, keepdims=True)
        for k, entry in enumerate((word_a, word_b, jnp.broadcast_to(used, (1, pairs)))):
            lists[3 * group + k : 3 * group + k + 1, :] = entry.astype(jnp.int32)

    wide = jnp.broadcast_to(order[...].astype(jnp.float32), (shots, shots))
    source[...] = jnp.broadcast_to(wide.T[:, :1], source.shape).astype(jnp.int32)


def picked_rows(value, source):
    groups = value.shape[0] // 8
    parts = []
    for i in range(groups):
        want = source[8 * i : 8 * i + 8]
        part = None
        for j in range(groups):
            found = jnp.take_along_axis(value[8 * j : 8 * j + 8], want & 7, axis=0)
            part = found if part is None else jnp.where(want >> 3 == j, found, part)
        parts.append(part)
    return jnp.concatenate(parts, axis=0)


def arrange(moves, down_tiles, up_tiles, weights):
    rows = lax.broadcasted_iota(jnp.int32, (TILE, TILE), 0)
    identity = (rows == lax.broadcasted_iota(jnp.int32, (TILE, TILE), 1)).astype(jnp.bfloat16)
    upward, _ = roles(moves)

    for t in range(weights.shape[0]):
        tile = jnp.where(upward, up_tiles[0, t], down_tiles[0, t])
        if t % 2:
            weights[t] = lax.dot_general(
                identity, tile, (((1,), (1,)), ((), ())), preferred_element_type=jnp.float32
            ).astype(jnp.bfloat16)
        else:
            weights[t] = tile.T


def split(block, columns):
    count = columns.shape[0] - 1
    for k in range(count):
        columns[k] = block[0, :, k * TILE:(k + 1) * TILE]
    columns[count] = jnp.zeros(columns.shape[1:], columns.dtype)


def add_products(lists, group, pairs, columns, weights, total):
    column_bits, tile_bits = bits(weights.shape[0], total.shape[0])
    column_mask, tile_mask = 2**column_bits - 1, 2**tile_bits - 1
    for p in range(*pairs):
        a, b = lists[3 * group, p], lists[3 * group + 1, p]
        read = jnp.concatenate([columns[a & column_mask], columns[b & column_mask]], axis=1)
        tile_a, tile_b = (a >> column_bits) & tile_mask, b >> column_bits
        both = jnp.concatenate([weights[tile_a], weights[tile_b]], axis=0)
        row = a >> (column_bits + tile_bits)
        total[row] += jnp.dot(read, both, preferred_element_type=jnp.float32)


def stage_kernel(moves, final, group, lists, source, block, weights, before, down, up, out, columns, total):
    count, pairs = total.shape[0], lists.shape[1]
    upward, _ = roles(moves)
    split(block, columns)
    for k in range(count):
        here = slice(k * TILE, (k + 1) * TILE)
        if before is None:
            total[k] = jnp.where(upward, up[0, :, here], down[0, :, here]).astype(jnp.float32)
        else:
            total[k] = before[k]

    def finish():
        for k in range(count):
            here = slice(k * TILE, (k + 1) * TILE)
            if group < 2:
                out[k] = total[k]
                continue
            fresh = total[k].astype(jnp.bfloat16)
            if final:
                rest = jnp.where(upward, down[0, :, here], up[0, :, here])
                both = (fresh.astype(jnp.float32) + rest.astype(jnp.float32)).astype(jnp.bfloat16)
                fresh = picked_rows(both.astype(jnp.float32), source[...]).astype(jnp.bfloat16)
            out[0, :, here] = fresh

    def run(*ends):
        add_products(lists, group, (0, ends[0]), columns, weights, total)
        finish()
        for low, high in zip(ends, ends[1:]):

            @pl.when(lists[3 * group + 2, 0] > low)
            def _(low=low, high=high):
                add_products(lists, group, (low, high), columns, weights, total)
                finish()

    some, many = -(-4 * pairs // 9), -(-7 * pairs // 9)
    if group == 0:
        run(pairs)
    elif group == 1:
        own_later = crosses(lax.axis_index("rows"))
        pl.when(own_later)(lambda: run(many, pairs))
        pl.when(jnp.logical_not(own_later))(lambda: run(some, pairs))
    else:
        run(some, pairs)


def step(moves, final, leaving, down, up, down_tiles, up_tiles, tile_rows, tile_cols, order):
    rows = lax.axis_size("rows")
    _, shots, width = down.shape
    tiles, count = tile_rows.shape[1], width // TILE
    pairs = (tiles + min(tiles, count)) // 2
    shape = jax.ShapeDtypeStruct
    sums = shape((count, shots, TILE), jnp.float32)
    scratch = [pltpu.VMEM((count + 1, shots, TILE), jnp.bfloat16), pltpu.VMEM(sums.shape, sums.dtype)]

    first, distant = across(leaving, moves, rows)
    lists, source, weights = call(
        functools.partial(prepare_kernel, moves, count),
        "prepare",
        (
            shape((9, pairs), jnp.int32),
            shape((shots, TILE), jnp.int32),
            shape((tiles, TILE, TILE), down_tiles.dtype),
        ),
    )(tile_rows, tile_cols, order, down_tiles, up_tiles)
    first, lists = lax.optimization_barrier((first, lists))
    second = lax.ppermute(first, "rows", [(r, partner(r, rows)) for r in range(rows)])

    def stage(group, block, before):
        def kernel(lists, source, block, weights, down, up, *others):
            before, others = (None, others) if group == 0 else (others[0], others[1:])
            stage_kernel(moves, final, group, lists, source, block, weights, before, down, up, *others)

        return call(
            kernel,
            ("first", "second", "far")[group],
            down if group == 2 else sums,
            scratch,
            flops=3 * 10**9 if group == 0 else 0,
        )(lists, source, block, weights, down, up, *([] if before is None else [before]))

    total = stage(0, first, None)
    total = stage(1, second, total)
    return stage(2, distant, total)


def shards(down_sources, up_sources, down_tiles, up_tiles, tile_rows, tile_cols, shot_order):
    layer = lax.axis_index("layer")
    order = shot_order.reshape(1, -1)
    steps = wavefront(lax.axis_size("layer"))
    down, up = down_sources, up_sources
    for at, moves in enumerate(steps):
        down_move, up_move = moves
        if up_move is None:
            leaving = down
        elif down_move is None:
            leaving = up
        else:
            leaving = jnp.where(layer == up_move[0], up, down)
        final = at == len(steps) - 1
        fresh = step(
            moves, final, leaving, down, up, down_tiles, up_tiles, tile_rows, tile_cols, order
        )
        if final:
            return fresh
        upward, _ = roles(moves)
        down, up = jnp.where(upward, down, fresh), jnp.where(upward, fresh, up)


def solution(mesh):
    return jax.shard_map(
        shards,
        mesh=mesh,
        in_specs=(
            P("layer", None, "rows"),
            P("layer", None, "rows"),
            P("layer", "rows", None, None),
            P("layer", "rows", None, None),
            P("layer", "rows"),
            P("layer", "rows"),
            P(),
        ),
        out_specs=P("layer", None, "rows"),
        check_vma=False,
    )
```

```python
import functools

import jax
import jax.numpy as jnp
from jax import lax
from jax.experimental import pallas as pl
from jax.experimental.pallas import tpu as pltpu
from jax.sharding import PartitionSpec as P

TILE = 128
VMEM_BYTES = 32 * 1024 * 1024


def wavefront(layers):
    steps = []
    for t in range(layers - 1):
        down, up = (t, t + 1), (layers - 1 - t, layers - 2 - t)
        if down[0] == up[0] or down[1] == up[1]:
            steps += [(down, None), (None, up)]
        else:
            steps.append((down, up))
    return steps


def partner(r, rows):
    other = r ^ 1
    return other if other < rows else r


def farther(r, rows):
    other = r + 1 if r % 2 else r - 1
    return other if 0 <= other < rows else r


def crosses(r):
    return r < 2


def across(block, held, moves, rows):
    moves = [m for m in moves if m is not None]
    axes = ("layer", "rows")
    first = [partner(r, rows) if crosses(r) else r for r in range(rows)]
    near = [(s * rows + r, d * rows + first[r]) for s, d in moves for r in range(rows)]
    far = [(s * rows + r, d * rows + farther(r, rows)) for s, d in moves for r in range(rows)]
    return lax.ppermute(block, axes, near), lax.ppermute(held, axes, far)


def pick(moves, down, up, small):
    down_move, up_move = moves
    half = down.shape[1] // 2

    def kernel(down, up, *others):
        small, out, small_out, sems = others[:count], others[count], others[count + 1 : -1], others[-1]

        def copies(source):
            return [
                pltpu.make_async_copy(
                    source.at[:, pl.ds(k * half, half)], out.at[:, pl.ds(k * half, half)], sems.at[k]
                )
                for k in range(2)
            ]

        def start(source):
            for copy in copies(source):
                copy.start()

        if up_move is None:
            start(down)
        elif down_move is None:
            start(up)
        else:
            upward = lax.axis_index("layer") == up_move[0]
            pl.when(upward)(lambda: start(up))
            pl.when(jnp.logical_not(upward))(lambda: start(down))
        rest = [
            pltpu.make_async_copy(there, here, sems.at[2 + k])
            for k, (there, here) in enumerate(zip(small, small_out))
        ]
        for copy in rest:
            copy.start()
        for copy in copies(down) + rest:
            copy.wait()

    count = len(small)
    scratch = [pltpu.SemaphoreType.DMA((2 + count,))]
    leaving, *small = call(kernel, "pick", (down, *small), scratch, outside=2 + count)(down, up, *small)
    return leaving, small


def hold(moves, block, down_tiles, up_tiles):
    def kernel(down_tiles, up_tiles, block, out, weights, tiles, sem):
        out[...] = block[...]

        @pl.when(last_row())
        def _():
            upward, _ = roles(moves)
            down_copy = pltpu.make_async_copy(down_tiles, tiles, sem)
            pl.when(upward)(lambda: pltpu.make_async_copy(up_tiles, tiles, sem).start())
            pl.when(jnp.logical_not(upward))(lambda: down_copy.start())
            down_copy.wait()
            transpose(tiles, weights)

    shape = jax.ShapeDtypeStruct
    return call(
        kernel,
        "hold",
        (block, shape(down_tiles.shape[1:], down_tiles.dtype)),
        [pltpu.VMEM(down_tiles.shape, down_tiles.dtype), pltpu.SemaphoreType.DMA],
        flops=3 * 10**9,
        outside=2,
    )(down_tiles, up_tiles, block)


def last_row():
    return lax.axis_index("rows") == lax.axis_size("rows") - 1


def transpose(tiles, weights):
    rows = lax.broadcasted_iota(jnp.int32, (TILE, TILE), 0)
    identity = (rows == lax.broadcasted_iota(jnp.int32, (TILE, TILE), 1)).astype(jnp.bfloat16)
    for t in range(weights.shape[0]):
        if t % 2:
            weights[t] = lax.dot_general(
                identity, tiles[0, t], (((1,), (1,)), ((), ())), preferred_element_type=jnp.float32
            ).astype(jnp.bfloat16)
        else:
            weights[t] = tiles[0, t].T


def call(kernel, name, out, scratch=(), flops=0, outside=0, aliases={}):
    vmem = pl.BlockSpec(memory_space=pltpu.VMEM)
    shapes = jax.tree.map(lambda leaf: jax.ShapeDtypeStruct(leaf.shape, leaf.dtype), out)

    def run(*operands):
        operands = [
            pltpu.with_memory_space_constraint(operand, pltpu.HBM) if k < outside else operand
            for k, operand in enumerate(operands)
        ]
        return pl.pallas_call(
            kernel,
            out_shape=shapes,
            in_specs=[pl.BlockSpec(memory_space=pl.ANY)] * outside + [vmem] * (len(operands) - outside),
            out_specs=jax.tree.map(lambda _: vmem, shapes),
            scratch_shapes=scratch,
            input_output_aliases=aliases,
            compiler_params=pltpu.CompilerParams(vmem_limit_bytes=VMEM_BYTES),
            cost_estimate=pl.CostEstimate(flops=flops, bytes_accessed=0, transcendentals=0),
            name=name,
        )(*operands)

    return run


def roles(moves):
    layer = lax.axis_index("layer")
    down_move, up_move = moves
    upward = layer == (up_move[1] if up_move else -1)
    downward = layer == (down_move[1] if down_move else -1)
    return upward, jnp.logical_or(upward, downward)


def bits(tiles, count):
    return count.bit_length(), (tiles - 1).bit_length()


def list_pairs(moves, count, tile_rows, tile_cols, order, lists, source):
    _, active = roles(moves)
    me = lax.axis_index("rows")
    n, shots = tile_rows.shape[1], source.shape[0]
    pairs = lists.shape[1] // 3
    column_bits, tile_bits = bits(n, count)
    even = me % 2 == 0
    row = tile_rows[...] - me * count
    seen = tile_cols[...] - (me - 1) * count
    far_start, beside_start = jnp.where(even, 0, 2 * count), jnp.where(even, 2 * count, 0)
    first_start = jnp.where(crosses(me), beside_start, count)
    far = (seen >= far_start) & (seen < far_start + count)
    first = (seen >= first_start) & (seen < first_start + count)
    group = jnp.where(far, 2, jnp.where(first, 0, 1))
    column = seen - jnp.where(seen < count, 0, jnp.where(seen < 2 * count, count, 2 * count))
    column = jnp.where(active, column, count)
    line = row + group * count
    line_l = jnp.broadcast_to(line.astype(jnp.float32), (n, n))
    both_s = (line_l * 2**column_bits + jnp.broadcast_to(column.astype(jnp.float32), (n, n))).T
    line_s = jnp.floor(both_s * 2.0**-column_bits)
    column_s = (both_s - line_s * 2**column_bits)[:, :1]
    t_l = lax.broadcasted_iota(jnp.int32, (n, n), 1)
    t_s = lax.broadcasted_iota(jnp.int32, (n, n), 0)
    same = line_l == line_s
    rank_l = jnp.sum(jnp.where(same & (t_s < t_l), 1.0, 0.0), axis=0, keepdims=True)
    rank_s = jnp.sum(jnp.where(same & (t_l < t_s), 1.0, 0.0), axis=1, keepdims=True)
    first_l = rank_l == 2.0 * jnp.floor(rank_l * 0.5)
    half_s = jnp.floor(rank_s * 0.5)
    first_s = rank_s == 2.0 * half_s
    group_s = jnp.where(line_s < count, 0.0, jnp.where(line_s < 2 * count, 1.0, 2.0))
    counted = (line_l < line_s) & (line_l >= group_s * count) & first_l
    ahead = jnp.sum(jnp.where(counted, 1.0, 0.0), axis=1, keepdims=True)
    slot = lax.broadcasted_iota(jnp.int32, (n, 3 * pairs), 1).astype(jnp.float32)
    hit = ahead + half_s + group_s[:, :1] * pairs == slot
    hit_a, hit_b = hit & first_s, hit & jnp.logical_not(first_s)

    def listed(hits, value):
        return jnp.sum(jnp.where(hits, value, 0.0), axis=0, keepdims=True).astype(jnp.int32)

    code_s = t_s[:, :1].astype(jnp.float32) * 2**column_bits + column_s - count
    row_s = (line_s - group_s * count)[:, :1] * 2 ** (column_bits + tile_bits)
    lists[0:1, :] = listed(hit_a, row_s + code_s) + count
    lists[1:2, :] = listed(hit_b, code_s) + count
    lists[2:3, :] = listed(hit_a, jnp.ones_like(code_s))

    wide = jnp.broadcast_to(order[...].astype(jnp.float32), (shots, shots))
    source[...] = jnp.broadcast_to(wide.T[:, :1], source.shape).astype(jnp.int32)


def picked_rows(value, source):
    groups = value.shape[0] // 8
    parts = []
    for i in range(groups):
        want = source[8 * i : 8 * i + 8]
        part = None
        for j in range(groups):
            found = jnp.take_along_axis(value[8 * j : 8 * j + 8], want & 7, axis=0)
            part = found if part is None else jnp.where(want >> 3 == j, found, part)
        parts.append(part)
    return jnp.concatenate(parts, axis=0)


def arrange_kernel(
    moves, far_rows, far_cols, far_order, down_tiles, up_tiles, held, weights, tile_rows, tile_cols, order, sems
):
    copies = [
        pltpu.make_async_copy(there, here, sems.at[k])
        for k, (there, here) in enumerate(
            ((far_rows, tile_rows), (far_cols, tile_cols), (far_order, order))
        )
    ]
    for copy in copies:
        copy.start()
    upward, _ = roles(moves)

    @pl.when(jnp.logical_not(last_row()))
    def _():
        pl.when(upward)(lambda: transpose(up_tiles, weights))
        pl.when(jnp.logical_not(upward))(lambda: transpose(down_tiles, weights))

    for copy in copies:
        copy.wait()


def split(block, columns):
    count = columns.shape[0] - 1
    for k in range(count):
        columns[k] = block[0, :, k * TILE:(k + 1) * TILE]
    columns[count] = jnp.zeros(columns.shape[1:], columns.dtype)


def add_products(lists, group, pairs, columns, weights, total):
    column_bits, tile_bits = bits(weights.shape[0], total.shape[0])
    column_mask, tile_mask = 2**column_bits - 1, 2**tile_bits - 1
    for p in range(*pairs):
        slot = group * (lists.shape[1] // 3) + p
        a, b = lists[0, slot], lists[1, slot]
        read = jnp.concatenate([columns[a & column_mask], columns[b & column_mask]], axis=1)
        tile_a, tile_b = (a >> column_bits) & tile_mask, b >> column_bits
        both = jnp.concatenate([weights[tile_a], weights[tile_b]], axis=0)
        row = a >> (column_bits + tile_bits)
        total[row] += jnp.dot(read, both, preferred_element_type=jnp.float32)


def stage_kernel(moves, final, group, lists, source, block, weights, before, down, up, out, columns, total):
    count, pairs = total.shape[0], lists.shape[1] // 3
    upward, _ = roles(moves)
    split(block, columns)
    for k in range(count):
        here = slice(k * TILE, (k + 1) * TILE)
        if before is None:
            total[k] = jnp.where(upward, up[0, :, here], down[0, :, here]).astype(jnp.float32)
        else:
            total[k] = before[k]

    def finish():
        for k in range(count):
            here = slice(k * TILE, (k + 1) * TILE)
            if group < 2:
                out[k] = total[k]
                continue
            fresh = total[k].astype(jnp.bfloat16)
            if final:
                rest = jnp.where(upward, down[0, :, here], up[0, :, here])
                both = (fresh.astype(jnp.float32) + rest.astype(jnp.float32)).astype(jnp.bfloat16)
                fresh = picked_rows(both.astype(jnp.float32), source[...]).astype(jnp.bfloat16)
            out[0, :, here] = fresh

    def run(*ends):
        add_products(lists, group, (0, ends[0]), columns, weights, total)
        finish()
        for low, high in zip(ends, ends[1:]):

            @pl.when(lists[2, group * pairs + low] > 0)
            def _(low=low, high=high):
                add_products(lists, group, (low, high), columns, weights, total)
                finish()

    some, many = -(-4 * pairs // 9), -(-7 * pairs // 9)
    if group == 0:
        run(pairs)
    elif group == 1:
        own_later = crosses(lax.axis_index("rows"))
        pl.when(own_later)(lambda: run(many, pairs))
        pl.when(jnp.logical_not(own_later))(lambda: run(some, pairs))
    else:
        run(some, pairs)


def step(moves, final, down, up, down_tiles, up_tiles, tile_rows, tile_cols, order):
    rows = lax.axis_size("rows")
    _, shots, width = down.shape
    tiles, count = tile_rows.shape[1], width // TILE
    pairs = (tiles + min(tiles, count)) // 2
    shape = jax.ShapeDtypeStruct
    sums = shape((count, shots, TILE), jnp.float32)
    scratch = [pltpu.VMEM((count + 1, shots, TILE), jnp.bfloat16), pltpu.VMEM(sums.shape, sums.dtype)]

    leaving, _ = pick(moves, down, up, ())
    held, weights = hold(moves, leaving, down_tiles, up_tiles)
    first, distant = across(leaving, held, moves, rows)
    weights, *small = call(
        functools.partial(arrange_kernel, moves),
        "arrange",
        (shape((tiles, TILE, TILE), down_tiles.dtype), tile_rows, tile_cols, order),
        [pltpu.SemaphoreType.DMA((3,))],
        outside=3,
        aliases={5: 0},
    )(tile_rows, tile_cols, order, down_tiles, up_tiles, weights)
    first, weights = lax.optimization_barrier((first, weights))
    second = lax.ppermute(first, "rows", [(r, partner(r, rows)) for r in range(rows)])

    def first_kernel(rows, cols, order, block, weights, down, up, out, lists, source, *scratch):
        list_pairs(moves, count, rows, cols, order, lists, source)
        stage_kernel(moves, final, 0, lists, source, block, weights, None, down, up, out, *scratch)

    total, lists, source = call(
        first_kernel,
        "first",
        (sums, shape((3, 3 * pairs), jnp.int32), shape((shots, TILE), jnp.int32)),
        scratch,
        flops=3 * 10**9,
    )(*small, first, weights, down, up)
    total = call(functools.partial(stage_kernel, moves, final, 1), "second", sums, scratch)(
        lists, source, second, weights, total, down, up
    )
    return call(functools.partial(stage_kernel, moves, final, 2), "far", down, scratch)(
        lists, source, distant, weights, total, down, up
    )


def shards(down_sources, up_sources, down_tiles, up_tiles, tile_rows, tile_cols, shot_order):
    order = shot_order.reshape(1, -1)
    steps = wavefront(lax.axis_size("layer"))
    down, up = down_sources, up_sources
    for at, moves in enumerate(steps):
        final = at == len(steps) - 1
        fresh = step(
            moves, final, down, up, down_tiles, up_tiles, tile_rows, tile_cols, order
        )
        if final:
            return fresh
        upward, _ = roles(moves)
        down, up = jnp.where(upward, down, fresh), jnp.where(upward, fresh, up)


def solution(mesh):
    return jax.shard_map(
        shards,
        mesh=mesh,
        in_specs=(
            P("layer", None, "rows"),
            P("layer", None, "rows"),
            P("layer", "rows", None, None),
            P("layer", "rows", None, None),
            P("layer", "rows"),
            P("layer", "rows"),
            P(),
        ),
        out_specs=P("layer", None, "rows"),
        check_vma=False,
    )
```

```python
import functools

import jax
import jax.numpy as jnp
from jax import lax
from jax.experimental import pallas as pl
from jax.experimental.pallas import tpu as pltpu
from jax.sharding import PartitionSpec as P

TILE = 128
VMEM_BYTES = 32 * 1024 * 1024


def wavefront(layers):
    steps = []
    for t in range(layers - 1):
        down, up = (t, t + 1), (layers - 1 - t, layers - 2 - t)
        if down[0] == up[0] or down[1] == up[1]:
            steps += [(down, None), (None, up)]
        else:
            steps.append((down, up))
    return steps


def partner(r, rows):
    other = r ^ 1
    return other if other < rows else r


def farther(r, rows):
    other = r + 1 if r % 2 else r - 1
    return other if 0 <= other < rows else r


def no_farther(r, rows):
    return (r == 0) | ((r == rows - 1) & (rows % 2 == 0))


def crosses(r):
    return r < 2


def across(block, held, moves, rows):
    moves = [m for m in moves if m is not None]
    axes = ("layer", "rows")
    first = [partner(r, rows) if crosses(r) else r for r in range(rows)]
    near = [(s * rows + r, d * rows + first[r]) for s, d in moves for r in range(rows)]
    far = [(s * rows + r, d * rows + farther(r, rows)) for s, d in moves for r in range(rows)]
    return lax.ppermute(block, axes, near), lax.ppermute(held, axes, far)


def pick(moves, down, up, small):
    down_move, up_move = moves
    half = down.shape[1] // 2

    def kernel(down, up, *others):
        small, out, small_out, sems = others[:count], others[count], others[count + 1 : -1], others[-1]

        def copies(source):
            return [
                pltpu.make_async_copy(
                    source.at[:, pl.ds(k * half, half)], out.at[:, pl.ds(k * half, half)], sems.at[k]
                )
                for k in range(2)
            ]

        def start(source):
            for copy in copies(source):
                copy.start()

        if up_move is None:
            start(down)
        elif down_move is None:
            start(up)
        else:
            upward = lax.axis_index("layer") == up_move[0]
            pl.when(upward)(lambda: start(up))
            pl.when(jnp.logical_not(upward))(lambda: start(down))
        rest = [
            pltpu.make_async_copy(there, here, sems.at[2 + k])
            for k, (there, here) in enumerate(zip(small, small_out))
        ]
        for copy in rest:
            copy.start()
        for copy in copies(down) + rest:
            copy.wait()

    count = len(small)
    scratch = [pltpu.SemaphoreType.DMA((2 + count,))]
    leaving, *small = call(kernel, "pick", (down, *small), scratch, outside=2 + count)(down, up, *small)
    return leaving, small


def hold(moves, block, down_tiles, up_tiles):
    def kernel(down_tiles, up_tiles, block, out, weights, tiles, sem):
        out[...] = block[...]

        @pl.when(last_row())
        def _():
            upward, _ = roles(moves)
            down_copy = pltpu.make_async_copy(down_tiles, tiles, sem)
            pl.when(upward)(lambda: pltpu.make_async_copy(up_tiles, tiles, sem).start())
            pl.when(jnp.logical_not(upward))(lambda: down_copy.start())
            down_copy.wait()
            transpose(tiles, weights)

    shape = jax.ShapeDtypeStruct
    return call(
        kernel,
        "hold",
        (block, shape(down_tiles.shape[1:], down_tiles.dtype)),
        [pltpu.VMEM(down_tiles.shape, down_tiles.dtype), pltpu.SemaphoreType.DMA],
        flops=3 * 10**9,
        outside=2,
    )(down_tiles, up_tiles, block)


def last_row():
    return lax.axis_index("rows") == lax.axis_size("rows") - 1


def transpose(tiles, weights):
    rows = lax.broadcasted_iota(jnp.int32, (TILE, TILE), 0)
    identity = (rows == lax.broadcasted_iota(jnp.int32, (TILE, TILE), 1)).astype(jnp.bfloat16)
    for t in range(weights.shape[0]):
        if t % 2:
            weights[t] = lax.dot_general(
                identity, tiles[0, t], (((1,), (1,)), ((), ())), preferred_element_type=jnp.float32
            ).astype(jnp.bfloat16)
        else:
            weights[t] = tiles[0, t].T


def call(kernel, name, out, scratch=(), flops=0, outside=0, aliases={}):
    vmem = pl.BlockSpec(memory_space=pltpu.VMEM)
    shapes = jax.tree.map(lambda leaf: jax.ShapeDtypeStruct(leaf.shape, leaf.dtype), out)

    def run(*operands):
        operands = [
            pltpu.with_memory_space_constraint(operand, pltpu.HBM) if k < outside else operand
            for k, operand in enumerate(operands)
        ]
        return pl.pallas_call(
            kernel,
            out_shape=shapes,
            in_specs=[pl.BlockSpec(memory_space=pl.ANY)] * outside + [vmem] * (len(operands) - outside),
            out_specs=jax.tree.map(lambda _: vmem, shapes),
            scratch_shapes=scratch,
            input_output_aliases=aliases,
            compiler_params=pltpu.CompilerParams(vmem_limit_bytes=VMEM_BYTES),
            cost_estimate=pl.CostEstimate(flops=flops, bytes_accessed=0, transcendentals=0),
            name=name,
        )(*operands)

    return run


def roles(moves):
    layer = lax.axis_index("layer")
    down_move, up_move = moves
    upward = layer == (up_move[1] if up_move else -1)
    downward = layer == (down_move[1] if down_move else -1)
    return upward, jnp.logical_or(upward, downward)


def bits(tiles, count):
    return count.bit_length(), (tiles - 1).bit_length()


def list_pairs(moves, count, tile_rows, tile_cols, order, lists, source):
    _, active = roles(moves)
    me = lax.axis_index("rows")
    n, shots = tile_rows.shape[1], source.shape[0]
    pairs = lists.shape[0] // 3
    column_bits, tile_bits = bits(n, count)
    even = me % 2 == 0
    row = tile_rows[...] - me * count
    seen = tile_cols[...] - (me - 1) * count
    far_start, beside_start = jnp.where(even, 0, 2 * count), jnp.where(even, 2 * count, 0)
    first_start = jnp.where(crosses(me), beside_start, count)
    far = (seen >= far_start) & (seen < far_start + count)
    first = (seen >= first_start) & (seen < first_start + count)
    group = jnp.where(far, 2, jnp.where(first, 0, 1))
    column = seen - jnp.where(seen < count, 0, jnp.where(seen < 2 * count, count, 2 * count))
    column = jnp.where(active, column, count)
    line = row + group * count
    line_l = jnp.broadcast_to(line.astype(jnp.float32), (n, n))
    both_s = (line_l * 2**column_bits + jnp.broadcast_to(column.astype(jnp.float32), (n, n))).T
    line_s = jnp.floor(both_s * 2.0**-column_bits)
    column_s = (both_s - line_s * 2**column_bits)[:, :1]
    t_l = lax.broadcasted_iota(jnp.int32, (n, n), 1)
    t_s = lax.broadcasted_iota(jnp.int32, (n, n), 0)
    same = line_l == line_s
    rank_l = jnp.sum(jnp.where(same & (t_s < t_l), 1.0, 0.0), axis=0, keepdims=True)
    rank_s = jnp.sum(jnp.where(same & (t_l < t_s), 1.0, 0.0), axis=1, keepdims=True)
    first_l = rank_l == 2.0 * jnp.floor(rank_l * 0.5)
    half_s = jnp.floor(rank_s * 0.5)
    first_s = rank_s == 2.0 * half_s
    group_s = jnp.where(line_s < count, 0.0, jnp.where(line_s < 2 * count, 1.0, 2.0))
    counted = (line_l < line_s) & (line_l >= group_s * count) & first_l
    ahead = jnp.sum(jnp.where(counted, 1.0, 0.0), axis=1, keepdims=True)
    slot = lax.broadcasted_iota(jnp.int32, (n, 3 * pairs), 1).astype(jnp.float32)
    hit = ahead + half_s + group_s[:, :1] * pairs == slot
    hit_a, hit_b = hit & first_s, hit & jnp.logical_not(first_s)

    def listed(hits, value):
        return jnp.sum(jnp.where(hits, value, 0.0), axis=0, keepdims=True)

    code_s = t_s[:, :1].astype(jnp.float32) * 2**column_bits + column_s - count
    row_s = (line_s - group_s * count)[:, :1] * 2 ** (column_bits + tile_bits)
    word = (listed(hit_a, row_s + code_s) + count) * 2 ** (column_bits + tile_bits)
    word = word + listed(hit_b, code_s) + count
    lists[...] = jnp.broadcast_to(word, (TILE, 3 * pairs)).T.astype(jnp.int32)

    wide = jnp.broadcast_to(order[...].astype(jnp.float32), (shots, shots))
    source[...] = jnp.broadcast_to(wide.T[:, :1], source.shape).astype(jnp.int32)


def picked_rows(value, source):
    groups = value.shape[0] // 8
    parts = []
    for i in range(groups):
        want = source[8 * i : 8 * i + 8]
        part = None
        for j in range(groups):
            found = jnp.take_along_axis(value[8 * j : 8 * j + 8], want & 7, axis=0)
            part = found if part is None else jnp.where(want >> 3 == j, found, part)
        parts.append(part)
    return jnp.concatenate(parts, axis=0)


def arrange_kernel(
    moves, far_rows, far_cols, far_order, down_tiles, up_tiles, held, weights, tile_rows, tile_cols, order, sems
):
    copies = [
        pltpu.make_async_copy(there, here, sems.at[k])
        for k, (there, here) in enumerate(
            ((far_rows, tile_rows), (far_cols, tile_cols), (far_order, order))
        )
    ]
    for copy in copies:
        copy.start()
    upward, _ = roles(moves)

    @pl.when(jnp.logical_not(last_row()))
    def _():
        pl.when(upward)(lambda: transpose(up_tiles, weights))
        pl.when(jnp.logical_not(upward))(lambda: transpose(down_tiles, weights))

    for copy in copies:
        copy.wait()


def split(block, columns):
    count = columns.shape[0] - 1
    for k in range(count):
        columns[k] = block[0, :, k * TILE:(k + 1) * TILE]
    columns[count] = jnp.zeros(columns.shape[1:], columns.dtype)


def add_products(lists, group, pairs, columns, weights, total):
    column_bits, tile_bits = bits(weights.shape[0], total.shape[0])
    column_mask, tile_mask = 2**column_bits - 1, 2**tile_bits - 1
    for p in range(*pairs):
        word = lists[group * (lists.shape[0] // 3) + p, 0]
        one = word >> (column_bits + tile_bits)
        read = jnp.concatenate([columns[one & column_mask], columns[word & column_mask]], axis=1)
        tiles = (one >> column_bits) & tile_mask, (word >> column_bits) & tile_mask
        both = jnp.concatenate([weights[tiles[0]], weights[tiles[1]]], axis=0)
        row = one >> (column_bits + tile_bits)
        total[row] += jnp.dot(read, both, preferred_element_type=jnp.float32)


def stage_kernel(moves, final, group, lists, source, block, weights, before, down, up, out, columns, total):
    count, pairs = total.shape[0], lists.shape[0] // 3
    upward, _ = roles(moves)
    column_bits, tile_bits = bits(weights.shape[0], count)
    split(block, columns)
    for k in range(count):
        here = slice(k * TILE, (k + 1) * TILE)
        if before is None:
            total[k] = jnp.where(upward, up[0, :, here], down[0, :, here]).astype(jnp.float32)
        else:
            total[k] = before[k]

    def finish():
        for k in range(count):
            here = slice(k * TILE, (k + 1) * TILE)
            if group < 2:
                out[k] = total[k]
                continue
            fresh = total[k].astype(jnp.bfloat16)
            if final:
                rest = jnp.where(upward, down[0, :, here], up[0, :, here])
                both = (fresh.astype(jnp.float32) + rest.astype(jnp.float32)).astype(jnp.bfloat16)
                fresh = picked_rows(both.astype(jnp.float32), source[...]).astype(jnp.bfloat16)
            out[0, :, here] = fresh

    def run(*ends):
        add_products(lists, group, (0, ends[0]), columns, weights, total)
        finish()
        for low, high in zip(ends, ends[1:]):

            column = lists[group * pairs + low, 0] >> (column_bits + tile_bits)

            @pl.when(column & (2**column_bits - 1) < count)
            def _(low=low, high=high):
                add_products(lists, group, (low, high), columns, weights, total)
                finish()

    some, many = -(-4 * pairs // 9), -(-7 * pairs // 9)
    if group == 0:
        run(pairs)
    elif group == 1:
        own_later = crosses(lax.axis_index("rows"))
        pl.when(own_later)(lambda: run(many, pairs))
        pl.when(jnp.logical_not(own_later))(lambda: run(some, pairs))
    else:
        alone = no_farther(lax.axis_index("rows"), lax.axis_size("rows"))
        pl.when(alone)(finish)
        pl.when(jnp.logical_not(alone))(lambda: run(some, pairs))


def step(moves, final, down, up, down_tiles, up_tiles, tile_rows, tile_cols, order):
    rows = lax.axis_size("rows")
    _, shots, width = down.shape
    tiles, count = tile_rows.shape[1], width // TILE
    pairs = (tiles + min(tiles, count)) // 2
    shape = jax.ShapeDtypeStruct
    sums = shape((count, shots, TILE), jnp.float32)
    scratch = [pltpu.VMEM((count + 1, shots, TILE), jnp.bfloat16), pltpu.VMEM(sums.shape, sums.dtype)]

    leaving, _ = pick(moves, down, up, ())
    held, weights = hold(moves, leaving, down_tiles, up_tiles)
    first, distant = across(leaving, held, moves, rows)
    weights, *small = call(
        functools.partial(arrange_kernel, moves),
        "arrange",
        (shape((tiles, TILE, TILE), down_tiles.dtype), tile_rows, tile_cols, order),
        [pltpu.SemaphoreType.DMA((3,))],
        outside=3,
        aliases={5: 0},
    )(tile_rows, tile_cols, order, down_tiles, up_tiles, weights)
    first, weights = lax.optimization_barrier((first, weights))
    second = lax.ppermute(first, "rows", [(r, partner(r, rows)) for r in range(rows)])

    def first_kernel(rows, cols, order, block, weights, down, up, out, lists, source, *scratch):
        list_pairs(moves, count, rows, cols, order, lists, source)
        stage_kernel(moves, final, 0, lists, source, block, weights, None, down, up, out, *scratch)

    total, lists, source = call(
        first_kernel,
        "first",
        (sums, shape((3 * pairs, TILE), jnp.int32), shape((shots, TILE), jnp.int32)),
        scratch,
        flops=3 * 10**9,
    )(*small, first, weights, down, up)
    total = call(functools.partial(stage_kernel, moves, final, 1), "second", sums, scratch)(
        lists, source, second, weights, total, down, up
    )
    return call(functools.partial(stage_kernel, moves, final, 2), "far", down, scratch)(
        lists, source, distant, weights, total, down, up
    )


def shards(down_sources, up_sources, down_tiles, up_tiles, tile_rows, tile_cols, shot_order):
    order = shot_order.reshape(1, -1)
    steps = wavefront(lax.axis_size("layer"))
    down, up = down_sources, up_sources
    for at, moves in enumerate(steps):
        final = at == len(steps) - 1
        fresh = step(
            moves, final, down, up, down_tiles, up_tiles, tile_rows, tile_cols, order
        )
        if final:
            return fresh
        upward, _ = roles(moves)
        down, up = jnp.where(upward, down, fresh), jnp.where(upward, fresh, up)


def solution(mesh):
    return jax.shard_map(
        shards,
        mesh=mesh,
        in_specs=(
            P("layer", None, "rows"),
            P("layer", None, "rows"),
            P("layer", "rows", None, None),
            P("layer", "rows", None, None),
            P("layer", "rows"),
            P("layer", "rows"),
            P(),
        ),
        out_specs=P("layer", None, "rows"),
        check_vma=False,
    )
```

```python
import functools

import jax
import jax.numpy as jnp
from jax import lax
from jax.experimental import pallas as pl
from jax.experimental.pallas import tpu as pltpu
from jax.sharding import PartitionSpec as P

TILE = 128
VMEM_BYTES = 32 * 1024 * 1024


def wavefront(layers):
    steps = []
    for t in range(layers - 1):
        down, up = (t, t + 1), (layers - 1 - t, layers - 2 - t)
        if down[0] == up[0] or down[1] == up[1]:
            steps += [(down, None), (None, up)]
        else:
            steps.append((down, up))
    return steps


def partner(r, rows):
    other = r ^ 1
    return other if other < rows else r


def farther(r, rows):
    other = r + 1 if r % 2 else r - 1
    return other if 0 <= other < rows else r


def no_farther(r, rows):
    return (r == 0) | ((r == rows - 1) & (rows % 2 == 0))


def across(block, held, moves, rows):
    moves = [m for m in moves if m is not None]
    axes = ("layer", "rows")
    near = [(s * rows + r, d * rows + r) for s, d in moves for r in range(rows)]
    far = [(s * rows + r, d * rows + farther(r, rows)) for s, d in moves for r in range(rows)]
    return lax.ppermute(block, axes, near), lax.ppermute(held, axes, far)


def pick(moves, down, up, small):
    down_move, up_move = moves
    half = down.shape[1] // 2

    def kernel(down, up, *others):
        small, out, small_out, sems = others[:count], others[count], others[count + 1 : -1], others[-1]

        def copies(source):
            return [
                pltpu.make_async_copy(
                    source.at[:, pl.ds(k * half, half)], out.at[:, pl.ds(k * half, half)], sems.at[k]
                )
                for k in range(2)
            ]

        def start(source):
            for copy in copies(source):
                copy.start()

        if up_move is None:
            start(down)
        elif down_move is None:
            start(up)
        else:
            upward = lax.axis_index("layer") == up_move[0]
            pl.when(upward)(lambda: start(up))
            pl.when(jnp.logical_not(upward))(lambda: start(down))
        rest = [
            pltpu.make_async_copy(there, here, sems.at[2 + k])
            for k, (there, here) in enumerate(zip(small, small_out))
        ]
        for copy in rest:
            copy.start()
        for copy in copies(down) + rest:
            copy.wait()

    count = len(small)
    scratch = [pltpu.SemaphoreType.DMA((2 + count,))]
    leaving, *small = call(kernel, "pick", (down, *small), scratch, outside=2 + count)(down, up, *small)
    return leaving, small


def hold(moves, block, down_tiles, up_tiles):
    def kernel(down_tiles, up_tiles, block, out, weights, tiles, sem):
        out[...] = block[...]

        @pl.when(last_row())
        def _():
            upward, _ = roles(moves)
            down_copy = pltpu.make_async_copy(down_tiles, tiles, sem)
            pl.when(upward)(lambda: pltpu.make_async_copy(up_tiles, tiles, sem).start())
            pl.when(jnp.logical_not(upward))(lambda: down_copy.start())
            down_copy.wait()
            transpose(tiles, weights)

    shape = jax.ShapeDtypeStruct
    return call(
        kernel,
        "hold",
        (block, shape(down_tiles.shape[1:], down_tiles.dtype)),
        [pltpu.VMEM(down_tiles.shape, down_tiles.dtype), pltpu.SemaphoreType.DMA],
        flops=3 * 10**9,
        outside=2,
    )(down_tiles, up_tiles, block)


def last_row():
    return lax.axis_index("rows") == lax.axis_size("rows") - 1


def transpose(tiles, weights):
    rows = lax.broadcasted_iota(jnp.int32, (TILE, TILE), 0)
    identity = (rows == lax.broadcasted_iota(jnp.int32, (TILE, TILE), 1)).astype(jnp.bfloat16)
    for t in range(weights.shape[0]):
        if t % 2:
            weights[t] = lax.dot_general(
                identity, tiles[0, t], (((1,), (1,)), ((), ())), preferred_element_type=jnp.float32
            ).astype(jnp.bfloat16)
        else:
            weights[t] = tiles[0, t].T


def call(kernel, name, out, scratch=(), flops=0, outside=0, outside_out=0, aliases={}):
    vmem = pl.BlockSpec(memory_space=pltpu.VMEM)
    shapes = jax.tree.map(lambda leaf: jax.ShapeDtypeStruct(leaf.shape, leaf.dtype), out)

    specs = jax.tree.map(lambda _: vmem, shapes)
    if outside_out:
        specs = tuple(pl.BlockSpec(memory_space=pl.ANY) if k < outside_out else vmem for k in range(len(shapes)))

    def run(*operands):
        operands = [
            pltpu.with_memory_space_constraint(operand, pltpu.HBM) if k < outside else operand
            for k, operand in enumerate(operands)
        ]
        return pl.pallas_call(
            kernel,
            out_shape=shapes,
            in_specs=[pl.BlockSpec(memory_space=pl.ANY)] * outside + [vmem] * (len(operands) - outside),
            out_specs=specs,
            scratch_shapes=scratch,
            input_output_aliases=aliases,
            compiler_params=pltpu.CompilerParams(vmem_limit_bytes=VMEM_BYTES),
            cost_estimate=pl.CostEstimate(flops=flops, bytes_accessed=0, transcendentals=0),
            name=name,
        )(*operands)

    return run


def roles(moves):
    layer = lax.axis_index("layer")
    down_move, up_move = moves
    upward = layer == (up_move[1] if up_move else -1)
    downward = layer == (down_move[1] if down_move else -1)
    return upward, jnp.logical_or(upward, downward)


def bits(tiles, count):
    return count.bit_length(), (tiles - 1).bit_length()


def list_pairs(moves, count, tile_rows, tile_cols, order, lists, source):
    _, active = roles(moves)
    me = lax.axis_index("rows")
    n, shots = tile_rows.shape[1], source.shape[0]
    pairs = lists.shape[0] // 3
    column_bits, tile_bits = bits(n, count)
    even = me % 2 == 0
    row = tile_rows[...] - me * count
    seen = tile_cols[...] - (me - 1) * count
    far_start = jnp.where(even, 0, 2 * count)
    far = (seen >= far_start) & (seen < far_start + count)
    own = (seen >= count) & (seen < 2 * count)
    group = jnp.where(far, 2, jnp.where(own, 0, 1))
    column = seen - jnp.where(seen < count, 0, jnp.where(seen < 2 * count, count, 2 * count))
    column = jnp.where(active, column, count)
    line = row + group * count
    line_l = jnp.broadcast_to(line.astype(jnp.float32), (n, n))
    both_s = (line_l * 2**column_bits + jnp.broadcast_to(column.astype(jnp.float32), (n, n))).T
    line_s = jnp.floor(both_s * 2.0**-column_bits)
    column_s = (both_s - line_s * 2**column_bits)[:, :1]
    t_l = lax.broadcasted_iota(jnp.int32, (n, n), 1)
    t_s = lax.broadcasted_iota(jnp.int32, (n, n), 0)
    same = line_l == line_s
    rank_l = jnp.sum(jnp.where(same & (t_s < t_l), 1.0, 0.0), axis=0, keepdims=True)
    rank_s = jnp.sum(jnp.where(same & (t_l < t_s), 1.0, 0.0), axis=1, keepdims=True)
    first_l = rank_l == 2.0 * jnp.floor(rank_l * 0.5)
    half_s = jnp.floor(rank_s * 0.5)
    first_s = rank_s == 2.0 * half_s
    group_s = jnp.where(line_s < count, 0.0, jnp.where(line_s < 2 * count, 1.0, 2.0))
    counted = (line_l < line_s) & (line_l >= group_s * count) & first_l
    ahead = jnp.sum(jnp.where(counted, 1.0, 0.0), axis=1, keepdims=True)
    slot = lax.broadcasted_iota(jnp.int32, (n, 3 * pairs), 1).astype(jnp.float32)
    hit = ahead + half_s + group_s[:, :1] * pairs == slot
    hit_a, hit_b = hit & first_s, hit & jnp.logical_not(first_s)

    def listed(hits, value):
        return jnp.sum(jnp.where(hits, value, 0.0), axis=0, keepdims=True)

    code_s = t_s[:, :1].astype(jnp.float32) * 2**column_bits + column_s - count
    row_s = (line_s - group_s * count)[:, :1] * 2 ** (column_bits + tile_bits)
    word = (listed(hit_a, row_s + code_s) + count) * 2 ** (column_bits + tile_bits)
    word = word + listed(hit_b, code_s) + count
    lists[...] = jnp.broadcast_to(word, (TILE, 3 * pairs)).T.astype(jnp.int32)

    wide = jnp.broadcast_to(order[...].astype(jnp.float32), (shots, shots))
    source[...] = jnp.broadcast_to(wide.T[:, :1], source.shape).astype(jnp.int32)


def picked_rows(value, source):
    groups = value.shape[0] // 8
    parts = []
    for i in range(groups):
        want = source[8 * i : 8 * i + 8]
        part = None
        for j in range(groups):
            found = jnp.take_along_axis(value[8 * j : 8 * j + 8], want & 7, axis=0)
            part = found if part is None else jnp.where(want >> 3 == j, found, part)
        parts.append(part)
    return jnp.concatenate(parts, axis=0)


def arrange_kernel(
    moves, far_rows, far_cols, far_order, down_tiles, up_tiles, held, weights, tile_rows, tile_cols, order, sems
):
    copies = [
        pltpu.make_async_copy(there, here, sems.at[k])
        for k, (there, here) in enumerate(
            ((far_rows, tile_rows), (far_cols, tile_cols), (far_order, order))
        )
    ]
    for copy in copies:
        copy.start()
    upward, _ = roles(moves)

    @pl.when(jnp.logical_not(last_row()))
    def _():
        pl.when(upward)(lambda: transpose(up_tiles, weights))
        pl.when(jnp.logical_not(upward))(lambda: transpose(down_tiles, weights))

    for copy in copies:
        copy.wait()


def split(block, columns):
    count = columns.shape[0] - 1
    for k in range(count):
        columns[k] = block[0, :, k * TILE:(k + 1) * TILE]
    columns[count] = jnp.zeros(columns.shape[1:], columns.dtype)


def add_products(lists, group, pairs, columns, weights, total):
    column_bits, tile_bits = bits(weights.shape[0], total.shape[0])
    column_mask, tile_mask = 2**column_bits - 1, 2**tile_bits - 1
    for p in range(*pairs):
        word = lists[group * (lists.shape[0] // 3) + p, 0]
        one = word >> (column_bits + tile_bits)
        read = jnp.concatenate([columns[one & column_mask], columns[word & column_mask]], axis=1)
        tiles = (one >> column_bits) & tile_mask, (word >> column_bits) & tile_mask
        both = jnp.concatenate([weights[tiles[0]], weights[tiles[1]]], axis=0)
        row = one >> (column_bits + tile_bits)
        total[row] += jnp.dot(read, both, preferred_element_type=jnp.float32)


def stage_kernel(moves, final, group, lists, source, block, weights, before, down, up, trace, out, columns, total, *rest):
    ready, sem = rest if group else (None, None)
    count, pairs = total.shape[0], lists.shape[0] // 3
    upward, _ = roles(moves)
    column_bits, tile_bits = bits(weights.shape[0], count)
    alone = no_farther(lax.axis_index("rows"), lax.axis_size("rows"))

    def load():
        split(block, columns)
        for k in range(count):
            here = slice(k * TILE, (k + 1) * TILE)
            if before is None:
                total[k] = jnp.where(upward, up[0, :, here], down[0, :, here]).astype(jnp.float32)
            else:
                total[k] = before[k]

    def complete():
        for k in range(count):
            here = slice(k * TILE, (k + 1) * TILE)
            fresh = total[k].astype(jnp.bfloat16)
            if final:
                other = jnp.where(upward, down[0, :, here], up[0, :, here])
                both = (fresh.astype(jnp.float32) + other.astype(jnp.float32)).astype(jnp.bfloat16)
                fresh = picked_rows(both.astype(jnp.float32), source[...]).astype(jnp.bfloat16)
            ready[0, :, here] = fresh
        pltpu.make_async_copy(ready, trace, sem).start()

    def complete_wait():
        pltpu.make_async_copy(ready, trace, sem).wait()

    usual = -(-4 * pairs // 9)

    def unusual(work):
        column = lists[group * pairs + usual, 0] >> (column_bits + tile_bits)

        @pl.when(column & (2**column_bits - 1) < count)
        def _():
            work()

    def add(low, high):
        add_products(lists, group, (low, high), columns, weights, total)

    if group == 0:
        load()
        add(0, pairs)
        out[...] = total[...]
    elif group == 1:
        load()
        add(0, usual)
        unusual(lambda: add(usual, pairs))
        out[...] = total[...]

        @pl.when(alone)
        def _():
            complete()
            complete_wait()
    else:

        @pl.when(jnp.logical_not(alone))
        def _():
            load()
            add(0, usual)
            complete()

            def more():
                complete_wait()
                add(usual, pairs)
                complete()

            unusual(more)
            complete_wait()


def step(moves, final, down, up, down_tiles, up_tiles, tile_rows, tile_cols, order):
    rows = lax.axis_size("rows")
    _, shots, width = down.shape
    tiles, count = tile_rows.shape[1], width // TILE
    pairs = (tiles + min(tiles, count)) // 2
    shape = jax.ShapeDtypeStruct
    sums = shape((count, shots, TILE), jnp.float32)
    scratch = [pltpu.VMEM((count + 1, shots, TILE), jnp.bfloat16), pltpu.VMEM(sums.shape, sums.dtype)]

    leaving, _ = pick(moves, down, up, ())
    held, weights = hold(moves, leaving, down_tiles, up_tiles)
    first, distant = across(leaving, held, moves, rows)
    weights, *small = call(
        functools.partial(arrange_kernel, moves),
        "arrange",
        (shape((tiles, TILE, TILE), down_tiles.dtype), tile_rows, tile_cols, order),
        [pltpu.SemaphoreType.DMA((3,))],
        outside=3,
        aliases={5: 0},
    )(tile_rows, tile_cols, order, down_tiles, up_tiles, weights)
    first, weights = lax.optimization_barrier((first, weights))
    second = lax.ppermute(first, "rows", [(r, partner(r, rows)) for r in range(rows)])

    def first_kernel(rows, cols, order, block, weights, down, up, out, lists, source, *scratch):
        list_pairs(moves, count, rows, cols, order, lists, source)
        stage_kernel(
            moves, final, 0, lists, source, block, weights, None, down, up, None, out, *scratch
        )

    def second_kernel(lists, source, block, weights, before, down, up, trace, out, *scratch):
        stage_kernel(
            moves, final, 1, lists, source, block, weights, before, down, up, trace, out, *scratch
        )

    def far_kernel(_, lists, source, block, weights, before, down, up, trace, *scratch):
        stage_kernel(
            moves, final, 2, lists, source, block, weights, before, down, up, trace, None, *scratch
        )

    total, lists, source = call(
        first_kernel,
        "first",
        (sums, shape((3 * pairs, TILE), jnp.int32), shape((shots, TILE), jnp.int32)),
        scratch,
        flops=3 * 10**9,
    )(*small, first, weights, down, up)
    scratch += [pltpu.VMEM(down.shape, down.dtype), pltpu.SemaphoreType.DMA]
    trace, total = call(second_kernel, "second", (down, sums), scratch, outside_out=1)(
        lists, source, second, weights, total, down, up
    )
    (trace,) = call(far_kernel, "far", (down,), scratch, outside=1, outside_out=1, aliases={0: 0})(
        trace, lists, source, distant, weights, total, down, up
    )
    return trace


def shards(down_sources, up_sources, down_tiles, up_tiles, tile_rows, tile_cols, shot_order):
    order = shot_order.reshape(1, -1)
    steps = wavefront(lax.axis_size("layer"))
    down, up = down_sources, up_sources
    for at, moves in enumerate(steps):
        final = at == len(steps) - 1
        fresh = step(
            moves, final, down, up, down_tiles, up_tiles, tile_rows, tile_cols, order
        )
        if final:
            return fresh
        upward, _ = roles(moves)
        down, up = jnp.where(upward, down, fresh), jnp.where(upward, fresh, up)


def solution(mesh):
    return jax.shard_map(
        shards,
        mesh=mesh,
        in_specs=(
            P("layer", None, "rows"),
            P("layer", None, "rows"),
            P("layer", "rows", None, None),
            P("layer", "rows", None, None),
            P("layer", "rows"),
            P("layer", "rows"),
            P(),
        ),
        out_specs=P("layer", None, "rows"),
        check_vma=False,
    )
```

```python
import functools

import jax
import jax.numpy as jnp
from jax import lax
from jax.experimental import pallas as pl
from jax.experimental.pallas import tpu as pltpu
from jax.sharding import PartitionSpec as P

TILE = 128
VMEM_BYTES = 32 * 1024 * 1024


def wavefront(layers):
    steps = []
    for t in range(layers - 1):
        down, up = (t, t + 1), (layers - 1 - t, layers - 2 - t)
        if down[0] == up[0] or down[1] == up[1]:
            steps += [(down, None), (None, up)]
        else:
            steps.append((down, up))
    return steps


def partner(r, rows):
    other = r ^ 1
    return other if other < rows else r


def farther(r, rows):
    other = r + 1 if r % 2 else r - 1
    return other if 0 <= other < rows else r


def no_farther(r, rows):
    return (r == 0) | ((r == rows - 1) & (rows % 2 == 0))


def across(block, held, moves, rows):
    moves = [m for m in moves if m is not None]
    axes = ("layer", "rows")
    near = [(s * rows + r, d * rows + r) for s, d in moves for r in range(rows)]
    far = [(s * rows + r, d * rows + farther(r, rows)) for s, d in moves for r in range(rows)]
    return lax.ppermute(block, axes, near), lax.ppermute(held, axes, far)


def pick(moves, down, up, small):
    down_move, up_move = moves
    half = down.shape[1] // 2

    def kernel(down, up, *others):
        small, out, small_out, sems = others[:count], others[count], others[count + 1 : -1], others[-1]

        def copies(source):
            return [
                pltpu.make_async_copy(
                    source.at[:, pl.ds(k * half, half)], out.at[:, pl.ds(k * half, half)], sems.at[k]
                )
                for k in range(2)
            ]

        def start(source):
            for copy in copies(source):
                copy.start()

        if up_move is None:
            start(down)
        elif down_move is None:
            start(up)
        else:
            upward = lax.axis_index("layer") == up_move[0]
            pl.when(upward)(lambda: start(up))
            pl.when(jnp.logical_not(upward))(lambda: start(down))
        rest = [
            pltpu.make_async_copy(there, here, sems.at[2 + k])
            for k, (there, here) in enumerate(zip(small, small_out))
        ]
        for copy in rest:
            copy.start()
        for copy in copies(down) + rest:
            copy.wait()

    count = len(small)
    scratch = [pltpu.SemaphoreType.DMA((2 + count,))]
    leaving, *small = call(kernel, "pick", (down, *small), scratch, outside=2 + count)(down, up, *small)
    return leaving, small


def hold(moves, block, down_tiles, up_tiles):
    def kernel(down_tiles, up_tiles, block, out, weights, tiles, sem):
        out[...] = block[...]

        @pl.when(last_row())
        def _():
            upward, _ = roles(moves)
            down_copy = pltpu.make_async_copy(down_tiles, tiles, sem)
            pl.when(upward)(lambda: pltpu.make_async_copy(up_tiles, tiles, sem).start())
            pl.when(jnp.logical_not(upward))(lambda: down_copy.start())
            down_copy.wait()
            transpose(tiles, weights)

    shape = jax.ShapeDtypeStruct
    return call(
        kernel,
        "hold",
        (block, shape(down_tiles.shape[1:], down_tiles.dtype)),
        [pltpu.VMEM(down_tiles.shape, down_tiles.dtype), pltpu.SemaphoreType.DMA],
        flops=3 * 10**9,
        outside=2,
    )(down_tiles, up_tiles, block)


def last_row():
    return lax.axis_index("rows") == lax.axis_size("rows") - 1


def transpose(tiles, weights):
    rows = lax.broadcasted_iota(jnp.int32, (TILE, TILE), 0)
    identity = (rows == lax.broadcasted_iota(jnp.int32, (TILE, TILE), 1)).astype(jnp.bfloat16)
    for t in range(weights.shape[0]):
        if t % 2:
            weights[t] = lax.dot_general(
                identity, tiles[0, t], (((1,), (1,)), ((), ())), preferred_element_type=jnp.float32
            ).astype(jnp.bfloat16)
        else:
            weights[t] = tiles[0, t].T


def call(kernel, name, out, scratch=(), flops=0, outside=0, outside_out=0, aliases={}):
    vmem = pl.BlockSpec(memory_space=pltpu.VMEM)
    shapes = jax.tree.map(lambda leaf: jax.ShapeDtypeStruct(leaf.shape, leaf.dtype), out)

    specs = jax.tree.map(lambda _: vmem, shapes)
    if outside_out:
        specs = tuple(pl.BlockSpec(memory_space=pl.ANY) if k < outside_out else vmem for k in range(len(shapes)))

    def run(*operands):
        operands = [
            pltpu.with_memory_space_constraint(operand, pltpu.HBM) if k < outside else operand
            for k, operand in enumerate(operands)
        ]
        return pl.pallas_call(
            kernel,
            out_shape=shapes,
            in_specs=[pl.BlockSpec(memory_space=pl.ANY)] * outside + [vmem] * (len(operands) - outside),
            out_specs=specs,
            scratch_shapes=scratch,
            input_output_aliases=aliases,
            compiler_params=pltpu.CompilerParams(vmem_limit_bytes=VMEM_BYTES),
            cost_estimate=pl.CostEstimate(flops=flops, bytes_accessed=0, transcendentals=0),
            name=name,
        )(*operands)

    return run


def roles(moves):
    layer = lax.axis_index("layer")
    down_move, up_move = moves
    upward = layer == (up_move[1] if up_move else -1)
    downward = layer == (down_move[1] if down_move else -1)
    return upward, jnp.logical_or(upward, downward)


def bits(tiles, count):
    return count.bit_length(), (tiles - 1).bit_length()


def list_pairs(moves, count, tile_rows, tile_cols, order, lists, source):
    _, active = roles(moves)
    me = lax.axis_index("rows")
    n, shots = tile_rows.shape[1], source.shape[0]
    pairs = lists.shape[0] // 3
    column_bits, tile_bits = bits(n, count)
    even = me % 2 == 0
    row = tile_rows[...] - me * count
    seen = tile_cols[...] - (me - 1) * count
    far_start = jnp.where(even, 0, 2 * count)
    far = (seen >= far_start) & (seen < far_start + count)
    own = (seen >= count) & (seen < 2 * count)
    group = jnp.where(far, 2, jnp.where(own, 0, 1))
    column = seen - jnp.where(seen < count, 0, jnp.where(seen < 2 * count, count, 2 * count))
    column = jnp.where(active, column, count)
    line = row + group * count
    line_l = jnp.broadcast_to(line.astype(jnp.float32), (n, n))
    both_s = (line_l * 2**column_bits + jnp.broadcast_to(column.astype(jnp.float32), (n, n))).T
    line_s = jnp.floor(both_s * 2.0**-column_bits)
    column_s = (both_s - line_s * 2**column_bits)[:, :1]
    t_l = lax.broadcasted_iota(jnp.int32, (n, n), 1)
    t_s = lax.broadcasted_iota(jnp.int32, (n, n), 0)
    same = line_l == line_s
    rank_l = jnp.sum(jnp.where(same & (t_s < t_l), 1.0, 0.0), axis=0, keepdims=True)
    rank_s = jnp.sum(jnp.where(same & (t_l < t_s), 1.0, 0.0), axis=1, keepdims=True)
    first_l = rank_l == 2.0 * jnp.floor(rank_l * 0.5)
    half_s = jnp.floor(rank_s * 0.5)
    first_s = rank_s == 2.0 * half_s
    group_s = jnp.where(line_s < count, 0.0, jnp.where(line_s < 2 * count, 1.0, 2.0))
    counted = (line_l < line_s) & (line_l >= group_s * count) & first_l
    ahead = jnp.sum(jnp.where(counted, 1.0, 0.0), axis=1, keepdims=True)
    slot = lax.broadcasted_iota(jnp.int32, (n, 3 * pairs), 1).astype(jnp.float32)
    hit = ahead + half_s + group_s[:, :1] * pairs == slot
    hit_a, hit_b = hit & first_s, hit & jnp.logical_not(first_s)

    def listed(hits, value):
        return jnp.sum(jnp.where(hits, value, 0.0), axis=0, keepdims=True)

    code_s = t_s[:, :1].astype(jnp.float32) * 2**column_bits + column_s - count
    row_s = (line_s - group_s * count)[:, :1] * 2 ** (column_bits + tile_bits)
    word = (listed(hit_a, row_s + code_s) + count) * 2 ** (column_bits + tile_bits)
    word = word + listed(hit_b, code_s) + count
    lists[...] = jnp.broadcast_to(word, (TILE, 3 * pairs)).T.astype(jnp.int32)

    wide = jnp.broadcast_to(order[...].astype(jnp.float32), (shots, shots))
    source[...] = jnp.broadcast_to(wide.T[:, :1], source.shape).astype(jnp.int32)


def picked_rows(value, source):
    groups = value.shape[0] // 8
    parts = []
    for i in range(groups):
        want = source[8 * i : 8 * i + 8]
        part = None
        for j in range(groups):
            found = jnp.take_along_axis(value[8 * j : 8 * j + 8], want & 7, axis=0)
            part = found if part is None else jnp.where(want >> 3 == j, found, part)
        parts.append(part)
    return jnp.concatenate(parts, axis=0)


def arrange_kernel(
    moves, far_rows, far_cols, far_order, down_tiles, up_tiles, held, weights, tile_rows, tile_cols, order, sems
):
    copies = [
        pltpu.make_async_copy(there, here, sems.at[k])
        for k, (there, here) in enumerate(
            ((far_rows, tile_rows), (far_cols, tile_cols), (far_order, order))
        )
    ]
    for copy in copies:
        copy.start()
    upward, _ = roles(moves)

    @pl.when(jnp.logical_not(last_row()))
    def _():
        pl.when(upward)(lambda: transpose(up_tiles, weights))
        pl.when(jnp.logical_not(upward))(lambda: transpose(down_tiles, weights))

    for copy in copies:
        copy.wait()


def add_products(lists, group, pairs, columns, weights, total):
    column_bits, tile_bits = bits(weights.shape[0], total.shape[0])
    column_mask, tile_mask = 2**column_bits - 1, 2**tile_bits - 1
    for p in range(*pairs):
        word = lists[group * (lists.shape[0] // 3) + p, 0]
        one = word >> (column_bits + tile_bits)
        read = jnp.concatenate([columns[one & column_mask], columns[word & column_mask]], axis=1)
        tiles = (one >> column_bits) & tile_mask, (word >> column_bits) & tile_mask
        both = jnp.concatenate([weights[tiles[0]], weights[tiles[1]]], axis=0)
        row = one >> (column_bits + tile_bits)
        total[row] += jnp.dot(read, both, preferred_element_type=jnp.float32)


def stage_kernel(
    moves, final, group, lists, source, block, weights, before, down, up, other, trace, out, columns, total, *rest
):
    ready, sem = rest if group else (None, None)
    count, pairs = total.shape[0], lists.shape[0] // 3
    upward, _ = roles(moves)
    column_bits, tile_bits = bits(weights.shape[0], count)
    alone = no_farther(lax.axis_index("rows"), lax.axis_size("rows"))

    def place(k):
        return slice(k * TILE, (k + 1) * TILE)

    def ordered(value):
        return picked_rows(value.astype(jnp.float32), source[...]) if final else value

    def load():
        for k in range(count):
            read = block[0, :, place(k)]
            columns[k] = ordered(read).astype(columns.dtype) if group == 2 else read
            if before is None:
                total[k] = jnp.where(upward, up[0, :, place(k)], down[0, :, place(k)]).astype(jnp.float32)
            else:
                total[k] = before[k]
        columns[count] = jnp.zeros(columns.shape[1:], columns.dtype)

    def complete(value, other):
        for k in range(count):
            fresh = value[k].astype(jnp.bfloat16)
            if final:
                fresh = (fresh.astype(jnp.float32) + other[k]).astype(jnp.bfloat16)
            ready[0, :, place(k)] = fresh
        pltpu.make_async_copy(ready, trace, sem).start()

    def complete_wait():
        pltpu.make_async_copy(ready, trace, sem).wait()

    usual = -(-4 * pairs // 9)

    def unusual(work):
        column = lists[group * pairs + usual, 0] >> (column_bits + tile_bits)

        @pl.when(column & (2**column_bits - 1) < count)
        def _():
            work()

    def add(low, high):
        add_products(lists, group, (low, high), columns, weights, total)

    if group == 0:
        load()
        add(0, pairs)
        out[...] = total[...]
    elif group == 1:
        load()
        add(0, usual)
        unusual(lambda: add(usual, pairs))
        for k in range(count):
            out[k] = ordered(total[k])
            if final:
                other[k] = ordered(jnp.where(upward, down[0, :, place(k)], up[0, :, place(k)]))

        @pl.when(alone)
        def _():
            complete(out, other)
            complete_wait()
    else:

        @pl.when(jnp.logical_not(alone))
        def _():
            load()
            add(0, usual)
            complete(total, other)

            def more():
                complete_wait()
                add(usual, pairs)
                complete(total, other)

            unusual(more)
            complete_wait()


def step(moves, final, down, up, down_tiles, up_tiles, tile_rows, tile_cols, order):
    rows = lax.axis_size("rows")
    _, shots, width = down.shape
    tiles, count = tile_rows.shape[1], width // TILE
    pairs = (tiles + min(tiles, count)) // 2
    shape = jax.ShapeDtypeStruct
    sums = shape((count, shots, TILE), jnp.float32)
    scratch = [pltpu.VMEM((count + 1, shots, TILE), jnp.bfloat16), pltpu.VMEM(sums.shape, sums.dtype)]

    leaving, _ = pick(moves, down, up, ())
    held, weights = hold(moves, leaving, down_tiles, up_tiles)
    first, distant = across(leaving, held, moves, rows)
    weights, *small = call(
        functools.partial(arrange_kernel, moves),
        "arrange",
        (shape((tiles, TILE, TILE), down_tiles.dtype), tile_rows, tile_cols, order),
        [pltpu.SemaphoreType.DMA((3,))],
        outside=3,
        aliases={5: 0},
    )(tile_rows, tile_cols, order, down_tiles, up_tiles, weights)
    first, weights = lax.optimization_barrier((first, weights))
    second = lax.ppermute(first, "rows", [(r, partner(r, rows)) for r in range(rows)])

    def first_kernel(rows, cols, order, block, weights, down, up, out, lists, source, *scratch):
        list_pairs(moves, count, rows, cols, order, lists, source)
        stage_kernel(
            moves, final, 0, lists, source, block, weights, None, down, up, None, None, out, *scratch
        )

    def second_kernel(lists, source, block, weights, before, down, up, trace, out, other, *scratch):
        stage_kernel(
            moves, final, 1, lists, source, block, weights, before, down, up, other, trace, out, *scratch
        )

    def far_kernel(_, lists, source, block, weights, before, other, trace, *scratch):
        stage_kernel(
            moves, final, 2, lists, source, block, weights, before, None, None, other, trace, None, *scratch
        )

    total, lists, source = call(
        first_kernel,
        "first",
        (sums, shape((3 * pairs, TILE), jnp.int32), shape((shots, TILE), jnp.int32)),
        scratch,
        flops=3 * 10**9,
    )(*small, first, weights, down, up)
    scratch += [pltpu.VMEM(down.shape, down.dtype), pltpu.SemaphoreType.DMA]
    trace, total, other = call(second_kernel, "second", (down, sums, sums), scratch, outside_out=1)(
        lists, source, second, weights, total, down, up
    )
    (trace,) = call(far_kernel, "far", (down,), scratch, outside=1, outside_out=1, aliases={0: 0})(
        trace, lists, source, distant, weights, total, other
    )
    return trace


def shards(down_sources, up_sources, down_tiles, up_tiles, tile_rows, tile_cols, shot_order):
    order = shot_order.reshape(1, -1)
    steps = wavefront(lax.axis_size("layer"))
    down, up = down_sources, up_sources
    for at, moves in enumerate(steps):
        final = at == len(steps) - 1
        fresh = step(
            moves, final, down, up, down_tiles, up_tiles, tile_rows, tile_cols, order
        )
        if final:
            return fresh
        upward, _ = roles(moves)
        down, up = jnp.where(upward, down, fresh), jnp.where(upward, fresh, up)


def solution(mesh):
    return jax.shard_map(
        shards,
        mesh=mesh,
        in_specs=(
            P("layer", None, "rows"),
            P("layer", None, "rows"),
            P("layer", "rows", None, None),
            P("layer", "rows", None, None),
            P("layer", "rows"),
            P("layer", "rows"),
            P(),
        ),
        out_specs=P("layer", None, "rows"),
        check_vma=False,
    )
```

```python
import functools

import jax
import jax.numpy as jnp
from jax import lax
from jax.experimental import pallas as pl
from jax.experimental.pallas import tpu as pltpu
from jax.sharding import PartitionSpec as P

TILE = 128
VMEM_BYTES = 32 * 1024 * 1024


def wavefront(layers):
    steps = []
    for t in range(layers - 1):
        down, up = (t, t + 1), (layers - 1 - t, layers - 2 - t)
        if down[0] == up[0] or down[1] == up[1]:
            steps += [(down, None), (None, up)]
        else:
            steps.append((down, up))
    return steps


def partner(r, rows):
    other = r ^ 1
    return other if other < rows else r


def farther(r, rows):
    other = r + 1 if r % 2 else r - 1
    return other if 0 <= other < rows else r


def no_farther(r, rows):
    return (r == 0) | ((r == rows - 1) & (rows % 2 == 0))


def across(block, held, moves, rows):
    moves = [m for m in moves if m is not None]
    axes = ("layer", "rows")
    near = [(s * rows + r, d * rows + r) for s, d in moves for r in range(rows)]
    far = [(s * rows + r, d * rows + farther(r, rows)) for s, d in moves for r in range(rows)]
    return lax.ppermute(block, axes, near), lax.ppermute(held, axes, far)


def pick(moves, down, up, small):
    down_move, up_move = moves
    half = down.shape[1] // 2

    def kernel(down, up, *others):
        small, out, small_out, sems = others[:count], others[count], others[count + 1 : -1], others[-1]

        def copies(source):
            return [
                pltpu.make_async_copy(
                    source.at[:, pl.ds(k * half, half)], out.at[:, pl.ds(k * half, half)], sems.at[k]
                )
                for k in range(2)
            ]

        def start(source):
            for copy in copies(source):
                copy.start()

        if up_move is None:
            start(down)
        elif down_move is None:
            start(up)
        else:
            upward = lax.axis_index("layer") == up_move[0]
            pl.when(upward)(lambda: start(up))
            pl.when(jnp.logical_not(upward))(lambda: start(down))
        rest = [
            pltpu.make_async_copy(there, here, sems.at[2 + k])
            for k, (there, here) in enumerate(zip(small, small_out))
        ]
        for copy in rest:
            copy.start()
        for copy in copies(down) + rest:
            copy.wait()

    count = len(small)
    scratch = [pltpu.SemaphoreType.DMA((2 + count,))]
    leaving, *small = call(kernel, "pick", (down, *small), scratch, outside=2 + count)(down, up, *small)
    return leaving, small


def hold(moves, block, down_tiles, up_tiles):
    def kernel(down_tiles, up_tiles, block, out, weights, tiles, sem):
        out[...] = block[...]

        @pl.when(last_row())
        def _():
            upward, _ = roles(moves)
            down_copy = pltpu.make_async_copy(down_tiles, tiles, sem)
            pl.when(upward)(lambda: pltpu.make_async_copy(up_tiles, tiles, sem).start())
            pl.when(jnp.logical_not(upward))(lambda: down_copy.start())
            down_copy.wait()
            transpose(tiles, weights)

    shape = jax.ShapeDtypeStruct
    return call(
        kernel,
        "hold",
        (block, shape(down_tiles.shape[1:], down_tiles.dtype)),
        [pltpu.VMEM(down_tiles.shape, down_tiles.dtype), pltpu.SemaphoreType.DMA],
        flops=3 * 10**9,
        outside=2,
    )(down_tiles, up_tiles, block)


def last_row():
    return lax.axis_index("rows") == lax.axis_size("rows") - 1


def transpose(tiles, weights):
    rows = lax.broadcasted_iota(jnp.int32, (TILE, TILE), 0)
    identity = (rows == lax.broadcasted_iota(jnp.int32, (TILE, TILE), 1)).astype(jnp.bfloat16)
    for t in range(weights.shape[0]):
        if t % 2:
            weights[t] = lax.dot_general(
                identity, tiles[0, t], (((1,), (1,)), ((), ())), preferred_element_type=jnp.float32
            ).astype(jnp.bfloat16)
        else:
            weights[t] = tiles[0, t].T


def call(kernel, name, out, scratch=(), flops=0, outside=0, outside_out=0, aliases={}):
    vmem = pl.BlockSpec(memory_space=pltpu.VMEM)
    shapes = jax.tree.map(lambda leaf: jax.ShapeDtypeStruct(leaf.shape, leaf.dtype), out)

    specs = jax.tree.map(lambda _: vmem, shapes)
    if outside_out:
        specs = tuple(pl.BlockSpec(memory_space=pl.ANY) if k < outside_out else vmem for k in range(len(shapes)))

    def run(*operands):
        operands = [
            pltpu.with_memory_space_constraint(operand, pltpu.HBM) if k < outside else operand
            for k, operand in enumerate(operands)
        ]
        return pl.pallas_call(
            kernel,
            out_shape=shapes,
            in_specs=[pl.BlockSpec(memory_space=pl.ANY)] * outside + [vmem] * (len(operands) - outside),
            out_specs=specs,
            scratch_shapes=scratch,
            input_output_aliases=aliases,
            compiler_params=pltpu.CompilerParams(vmem_limit_bytes=VMEM_BYTES),
            cost_estimate=pl.CostEstimate(flops=flops, bytes_accessed=0, transcendentals=0),
            name=name,
        )(*operands)

    return run


def roles(moves):
    layer = lax.axis_index("layer")
    down_move, up_move = moves
    upward = layer == (up_move[1] if up_move else -1)
    downward = layer == (down_move[1] if down_move else -1)
    return upward, jnp.logical_or(upward, downward)


def bits(tiles, count):
    return count.bit_length(), (tiles - 1).bit_length()


def list_pairs(moves, count, tile_rows, tile_cols, order, lists, source):
    _, active = roles(moves)
    me = lax.axis_index("rows")
    n, shots = tile_rows.shape[1], source.shape[0]
    pairs = lists.shape[0] // 3
    column_bits, tile_bits = bits(n, count)
    even = me % 2 == 0
    row = tile_rows[...] - me * count
    seen = tile_cols[...] - (me - 1) * count
    far_start = jnp.where(even, 0, 2 * count)
    far = (seen >= far_start) & (seen < far_start + count)
    own = (seen >= count) & (seen < 2 * count)
    group = jnp.where(far, 2, jnp.where(own, 0, 1))
    column = seen - jnp.where(seen < count, 0, jnp.where(seen < 2 * count, count, 2 * count))
    column = jnp.where(active, column, count)
    line = row + group * count
    line_l = jnp.broadcast_to(line.astype(jnp.float32), (n, n))
    both_s = (line_l * 2**column_bits + jnp.broadcast_to(column.astype(jnp.float32), (n, n))).T
    line_s = jnp.floor(both_s * 2.0**-column_bits)
    column_s = (both_s - line_s * 2**column_bits)[:, :1]
    t_l = lax.broadcasted_iota(jnp.int32, (n, n), 1)
    t_s = lax.broadcasted_iota(jnp.int32, (n, n), 0)
    same = line_l == line_s
    rank_l = jnp.sum(jnp.where(same & (t_s < t_l), 1.0, 0.0), axis=0, keepdims=True)
    rank_s = jnp.sum(jnp.where(same & (t_l < t_s), 1.0, 0.0), axis=1, keepdims=True)
    first_l = rank_l == 2.0 * jnp.floor(rank_l * 0.5)
    half_s = jnp.floor(rank_s * 0.5)
    first_s = rank_s == 2.0 * half_s
    group_s = jnp.where(line_s < count, 0.0, jnp.where(line_s < 2 * count, 1.0, 2.0))
    counted = (line_l < line_s) & (line_l >= group_s * count) & first_l
    ahead = jnp.sum(jnp.where(counted, 1.0, 0.0), axis=1, keepdims=True)
    slot = lax.broadcasted_iota(jnp.int32, (n, 3 * pairs), 1).astype(jnp.float32)
    hit = ahead + half_s + group_s[:, :1] * pairs == slot
    hit_a, hit_b = hit & first_s, hit & jnp.logical_not(first_s)

    def listed(hits, value):
        return jnp.sum(jnp.where(hits, value, 0.0), axis=0, keepdims=True)

    code_s = t_s[:, :1].astype(jnp.float32) * 2**column_bits + column_s - count
    row_s = (line_s - group_s * count)[:, :1] * 2 ** (column_bits + tile_bits)
    word = (listed(hit_a, row_s + code_s) + count) * 2 ** (column_bits + tile_bits)
    word = word + listed(hit_b, code_s) + count
    lists[...] = jnp.broadcast_to(word, (TILE, 3 * pairs)).T.astype(jnp.int32)

    wide = jnp.broadcast_to(order[...].astype(jnp.float32), (shots, shots))
    source[...] = jnp.broadcast_to(wide.T[:, :1], source.shape).astype(jnp.int32)


def picked_rows(value, source):
    groups = value.shape[0] // 8
    parts = []
    for i in range(groups):
        want = source[8 * i : 8 * i + 8]
        part = None
        for j in range(groups):
            found = jnp.take_along_axis(value[8 * j : 8 * j + 8], want & 7, axis=0)
            part = found if part is None else jnp.where(want >> 3 == j, found, part)
        parts.append(part)
    return jnp.concatenate(parts, axis=0)


def arrange_kernel(
    moves, far_rows, far_cols, far_order, down_tiles, up_tiles, held, weights, tile_rows, tile_cols, order, sems
):
    copies = [
        pltpu.make_async_copy(there, here, sems.at[k])
        for k, (there, here) in enumerate(
            ((far_rows, tile_rows), (far_cols, tile_cols), (far_order, order))
        )
    ]
    for copy in copies:
        copy.start()
    upward, _ = roles(moves)

    @pl.when(last_row())
    def _():
        weights[...] = held[...]

    @pl.when(jnp.logical_not(last_row()))
    def _():
        pl.when(upward)(lambda: transpose(up_tiles, weights))
        pl.when(jnp.logical_not(upward))(lambda: transpose(down_tiles, weights))

    for copy in copies:
        copy.wait()


def add_products(lists, group, pairs, columns, weights, total):
    column_bits, tile_bits = bits(weights.shape[0], total.shape[0])
    column_mask, tile_mask = 2**column_bits - 1, 2**tile_bits - 1
    for p in range(*pairs):
        word = lists[group * (lists.shape[0] // 3) + p, 0]
        one = word >> (column_bits + tile_bits)
        read = jnp.concatenate([columns[one & column_mask], columns[word & column_mask]], axis=1)
        tiles = (one >> column_bits) & tile_mask, (word >> column_bits) & tile_mask
        both = jnp.concatenate([weights[tiles[0]], weights[tiles[1]]], axis=0)
        row = one >> (column_bits + tile_bits)
        total[row] += jnp.dot(read, both, preferred_element_type=jnp.float32)


def stage_kernel(
    moves, final, group, lists, source, block, weights, before, down, up, other, trace, out, columns, total, *rest
):
    ready, sem = rest if group else (None, None)
    count, pairs = total.shape[0], lists.shape[0] // 3
    upward, _ = roles(moves)
    column_bits, tile_bits = bits(weights.shape[0], count)
    alone = no_farther(lax.axis_index("rows"), lax.axis_size("rows"))

    def place(k):
        return slice(k * TILE, (k + 1) * TILE)

    def ordered(value):
        return picked_rows(value.astype(jnp.float32), source[...]) if final else value

    def load():
        for k in range(count):
            read = block[0, :, place(k)]
            columns[k] = ordered(read).astype(columns.dtype) if group == 2 else read
            if before is None:
                total[k] = jnp.where(upward, up[0, :, place(k)], down[0, :, place(k)]).astype(jnp.float32)
            else:
                total[k] = before[k]
        columns[count] = jnp.zeros(columns.shape[1:], columns.dtype)

    def complete(value, other):
        for k in range(count):
            fresh = value[k].astype(jnp.bfloat16)
            if final:
                fresh = (fresh.astype(jnp.float32) + other[k]).astype(jnp.bfloat16)
            ready[0, :, place(k)] = fresh
        pltpu.make_async_copy(ready, trace, sem).start()

    def complete_wait():
        pltpu.make_async_copy(ready, trace, sem).wait()

    usual = -(-4 * pairs // 9)

    def unusual(work):
        column = lists[group * pairs + usual, 0] >> (column_bits + tile_bits)

        @pl.when(column & (2**column_bits - 1) < count)
        def _():
            work()

    def add(low, high):
        add_products(lists, group, (low, high), columns, weights, total)

    if group == 0:
        load()
        add(0, pairs)
        out[...] = total[...]
    elif group == 1:
        load()
        add(0, usual)
        unusual(lambda: add(usual, pairs))
        for k in range(count):
            out[k] = ordered(total[k])
            if final:
                other[k] = ordered(jnp.where(upward, down[0, :, place(k)], up[0, :, place(k)]))

        @pl.when(alone)
        def _():
            complete(out, other)
            complete_wait()
    else:

        @pl.when(jnp.logical_not(alone))
        def _():
            load()
            add(0, usual)
            complete(total, other)

            def more():
                complete_wait()
                add(usual, pairs)
                complete(total, other)

            unusual(more)
            complete_wait()


def step(moves, final, down, up, down_tiles, up_tiles, tile_rows, tile_cols, order):
    rows = lax.axis_size("rows")
    _, shots, width = down.shape
    tiles, count = tile_rows.shape[1], width // TILE
    pairs = (tiles + min(tiles, count)) // 2
    shape = jax.ShapeDtypeStruct
    sums = shape((count, shots, TILE), jnp.float32)
    scratch = [pltpu.VMEM((count + 1, shots, TILE), jnp.bfloat16), pltpu.VMEM(sums.shape, sums.dtype)]

    leaving, _ = pick(moves, down, up, ())
    held, weights = hold(moves, leaving, down_tiles, up_tiles)
    first, distant = across(leaving, held, moves, rows)
    weights, *small = call(
        functools.partial(arrange_kernel, moves),
        "arrange",
        (shape((tiles, TILE, TILE), down_tiles.dtype), tile_rows, tile_cols, order),
        [pltpu.SemaphoreType.DMA((3,))],
        outside=3,
    )(tile_rows, tile_cols, order, down_tiles, up_tiles, weights)
    first, weights = lax.optimization_barrier((first, weights))
    second = lax.ppermute(first, "rows", [(r, partner(r, rows)) for r in range(rows)])

    def first_kernel(rows, cols, order, block, weights, down, up, out, lists, source, *scratch):
        list_pairs(moves, count, rows, cols, order, lists, source)
        stage_kernel(
            moves, final, 0, lists, source, block, weights, None, down, up, None, None, out, *scratch
        )

    def second_kernel(lists, source, block, weights, before, down, up, trace, out, other, *scratch):
        stage_kernel(
            moves, final, 1, lists, source, block, weights, before, down, up, other, trace, out, *scratch
        )

    def far_kernel(_, lists, source, block, weights, before, other, trace, *scratch):
        stage_kernel(
            moves, final, 2, lists, source, block, weights, before, None, None, other, trace, None, *scratch
        )

    total, lists, source = call(
        first_kernel,
        "first",
        (sums, shape((3 * pairs, TILE), jnp.int32), shape((shots, TILE), jnp.int32)),
        scratch,
        flops=3 * 10**9,
    )(*small, first, weights, down, up)
    scratch += [pltpu.VMEM(down.shape, down.dtype), pltpu.SemaphoreType.DMA]
    trace, total, other = call(second_kernel, "second", (down, sums, sums), scratch, outside_out=1)(
        lists, source, second, weights, total, down, up
    )
    (trace,) = call(far_kernel, "far", (down,), scratch, outside=1, outside_out=1, aliases={0: 0})(
        trace, lists, source, distant, weights, total, other
    )
    return trace


def shards(down_sources, up_sources, down_tiles, up_tiles, tile_rows, tile_cols, shot_order):
    order = shot_order.reshape(1, -1)
    steps = wavefront(lax.axis_size("layer"))
    down, up = down_sources, up_sources
    for at, moves in enumerate(steps):
        final = at == len(steps) - 1
        fresh = step(
            moves, final, down, up, down_tiles, up_tiles, tile_rows, tile_cols, order
        )
        if final:
            return fresh
        upward, _ = roles(moves)
        down, up = jnp.where(upward, down, fresh), jnp.where(upward, fresh, up)


def solution(mesh):
    return jax.shard_map(
        shards,
        mesh=mesh,
        in_specs=(
            P("layer", None, "rows"),
            P("layer", None, "rows"),
            P("layer", "rows", None, None),
            P("layer", "rows", None, None),
            P("layer", "rows"),
            P("layer", "rows"),
            P(),
        ),
        out_specs=P("layer", None, "rows"),
        check_vma=False,
    )
```

```python
import functools

import jax
import jax.numpy as jnp
from jax import lax
from jax.experimental import pallas as pl
from jax.experimental.pallas import tpu as pltpu
from jax.sharding import PartitionSpec as P

TILE = 128
VMEM_BYTES = 32 * 1024 * 1024


def wavefront(layers):
    steps = []
    for t in range(layers - 1):
        down, up = (t, t + 1), (layers - 1 - t, layers - 2 - t)
        if down[0] == up[0] or down[1] == up[1]:
            steps += [(down, None), (None, up)]
        else:
            steps.append((down, up))
    return steps


def partner(r, rows):
    other = r ^ 1
    return other if other < rows else r


def farther(r, rows):
    other = r + 1 if r % 2 else r - 1
    return other if 0 <= other < rows else r


def no_farther(r, rows):
    return (r == 0) | ((r == rows - 1) & (rows % 2 == 0))


def across(block, held, moves, rows):
    moves = [m for m in moves if m is not None]
    axes = ("layer", "rows")
    near = [(s * rows + r, d * rows + r) for s, d in moves for r in range(rows)]
    far = [(s * rows + r, d * rows + farther(r, rows)) for s, d in moves for r in range(rows)]
    return lax.ppermute(block, axes, near), lax.ppermute(held, axes, far)


def pick(moves, down, up, small):
    down_move, up_move = moves
    half = down.shape[1] // 2

    def kernel(down, up, *others):
        small, out, small_out, sems = others[:count], others[count], others[count + 1 : -1], others[-1]

        def copies(source):
            return [
                pltpu.make_async_copy(
                    source.at[:, pl.ds(k * half, half)], out.at[:, pl.ds(k * half, half)], sems.at[k]
                )
                for k in range(2)
            ]

        def start(source):
            for copy in copies(source):
                copy.start()

        if up_move is None:
            start(down)
        elif down_move is None:
            start(up)
        else:
            upward = lax.axis_index("layer") == up_move[0]
            pl.when(upward)(lambda: start(up))
            pl.when(jnp.logical_not(upward))(lambda: start(down))
        rest = [
            pltpu.make_async_copy(there, here, sems.at[2 + k])
            for k, (there, here) in enumerate(zip(small, small_out))
        ]
        for copy in rest:
            copy.start()
        for copy in copies(down) + rest:
            copy.wait()

    count = len(small)
    scratch = [pltpu.SemaphoreType.DMA((2 + count,))]
    leaving, *small = call(kernel, "pick", (down, *small), scratch, outside=2 + count)(down, up, *small)
    return leaving, small


def hold(moves, block, down_tiles, up_tiles):
    def kernel(down_tiles, up_tiles, block, out, weights, tiles, sem):
        out[...] = block[...]

        @pl.when(last_row())
        def _():
            upward, _ = roles(moves)
            down_copy = pltpu.make_async_copy(down_tiles, tiles, sem)
            pl.when(upward)(lambda: pltpu.make_async_copy(up_tiles, tiles, sem).start())
            pl.when(jnp.logical_not(upward))(lambda: down_copy.start())
            down_copy.wait()
            transpose(tiles, weights)

    shape = jax.ShapeDtypeStruct
    return call(
        kernel,
        "hold",
        (block, shape(down_tiles.shape[1:], down_tiles.dtype)),
        [pltpu.VMEM(down_tiles.shape, down_tiles.dtype), pltpu.SemaphoreType.DMA],
        flops=3 * 10**9,
        outside=2,
    )(down_tiles, up_tiles, block)


def last_row():
    return lax.axis_index("rows") == lax.axis_size("rows") - 1


def transpose(tiles, weights):
    rows = lax.broadcasted_iota(jnp.int32, (TILE, TILE), 0)
    identity = (rows == lax.broadcasted_iota(jnp.int32, (TILE, TILE), 1)).astype(jnp.bfloat16)
    for t in range(weights.shape[0]):
        if t % 2:
            weights[t] = lax.dot_general(
                identity, tiles[0, t], (((1,), (1,)), ((), ())), preferred_element_type=jnp.float32
            ).astype(jnp.bfloat16)
        else:
            weights[t] = tiles[0, t].T


def call(kernel, name, out, scratch=(), flops=0, outside=0, outside_out=0, aliases={}):
    vmem = pl.BlockSpec(memory_space=pltpu.VMEM)
    shapes = jax.tree.map(lambda leaf: jax.ShapeDtypeStruct(leaf.shape, leaf.dtype), out)

    specs = jax.tree.map(lambda _: vmem, shapes)
    if outside_out:
        specs = tuple(pl.BlockSpec(memory_space=pl.ANY) if k < outside_out else vmem for k in range(len(shapes)))

    def run(*operands):
        operands = [
            pltpu.with_memory_space_constraint(operand, pltpu.HBM) if k < outside else operand
            for k, operand in enumerate(operands)
        ]
        return pl.pallas_call(
            kernel,
            out_shape=shapes,
            in_specs=[pl.BlockSpec(memory_space=pl.ANY)] * outside + [vmem] * (len(operands) - outside),
            out_specs=specs,
            scratch_shapes=scratch,
            input_output_aliases=aliases,
            compiler_params=pltpu.CompilerParams(vmem_limit_bytes=VMEM_BYTES),
            cost_estimate=pl.CostEstimate(flops=flops, bytes_accessed=0, transcendentals=0),
            name=name,
        )(*operands)

    return run


def roles(moves):
    layer = lax.axis_index("layer")
    down_move, up_move = moves
    upward = layer == (up_move[1] if up_move else -1)
    downward = layer == (down_move[1] if down_move else -1)
    return upward, jnp.logical_or(upward, downward)


def bits(tiles, count):
    return count.bit_length(), (tiles - 1).bit_length()


def list_pairs(moves, count, tile_rows, tile_cols, order, lists, source):
    _, active = roles(moves)
    me = lax.axis_index("rows")
    n, shots = tile_rows.shape[1], source.shape[0]
    pairs = lists.shape[0] // 3
    column_bits, tile_bits = bits(n, count)
    even = me % 2 == 0
    row = tile_rows[...] - me * count
    seen = tile_cols[...] - (me - 1) * count
    far_start = jnp.where(even, 0, 2 * count)
    far = (seen >= far_start) & (seen < far_start + count)
    own = (seen >= count) & (seen < 2 * count)
    group = jnp.where(far, 2, jnp.where(own, 0, 1))
    column = seen - jnp.where(seen < count, 0, jnp.where(seen < 2 * count, count, 2 * count))
    column = jnp.where(active, column, count)
    line = row + group * count
    line_l = jnp.broadcast_to(line.astype(jnp.float32), (n, n))
    both_s = (line_l * 2**column_bits + jnp.broadcast_to(column.astype(jnp.float32), (n, n))).T
    line_s = jnp.floor(both_s * 2.0**-column_bits)
    column_s = (both_s - line_s * 2**column_bits)[:, :1]
    t_l = lax.broadcasted_iota(jnp.int32, (n, n), 1)
    t_s = lax.broadcasted_iota(jnp.int32, (n, n), 0)
    same = line_l == line_s
    rank_l = jnp.sum(jnp.where(same & (t_s < t_l), 1.0, 0.0), axis=0, keepdims=True)
    rank_s = jnp.sum(jnp.where(same & (t_l < t_s), 1.0, 0.0), axis=1, keepdims=True)
    first_l = rank_l == 2.0 * jnp.floor(rank_l * 0.5)
    half_s = jnp.floor(rank_s * 0.5)
    first_s = rank_s == 2.0 * half_s
    group_s = jnp.where(line_s < count, 0.0, jnp.where(line_s < 2 * count, 1.0, 2.0))
    counted = (line_l < line_s) & (line_l >= group_s * count) & first_l
    ahead = jnp.sum(jnp.where(counted, 1.0, 0.0), axis=1, keepdims=True)
    slot = lax.broadcasted_iota(jnp.int32, (n, 3 * pairs), 1).astype(jnp.float32)
    hit = ahead + half_s + group_s[:, :1] * pairs == slot
    hit_a, hit_b = hit & first_s, hit & jnp.logical_not(first_s)

    def listed(hits, value):
        return jnp.sum(jnp.where(hits, value, 0.0), axis=0, keepdims=True)

    code_s = t_s[:, :1].astype(jnp.float32) * 2**column_bits + column_s - count
    row_s = (line_s - group_s * count)[:, :1] * 2 ** (column_bits + tile_bits)
    word = (listed(hit_a, row_s + code_s) + count) * 2 ** (column_bits + tile_bits)
    word = word + listed(hit_b, code_s) + count
    lists[...] = jnp.broadcast_to(word, (TILE, 3 * pairs)).T.astype(jnp.int32)

    wide = jnp.broadcast_to(order[...].astype(jnp.float32), (shots, shots))
    source[...] = jnp.broadcast_to(wide.T[:, :1], source.shape).astype(jnp.int32)


def picked_rows(value, source):
    groups = value.shape[0] // 8
    parts = []
    for i in range(groups):
        want = source[8 * i : 8 * i + 8]
        part = None
        for j in range(groups):
            found = jnp.take_along_axis(value[8 * j : 8 * j + 8], want & 7, axis=0)
            part = found if part is None else jnp.where(want >> 3 == j, found, part)
        parts.append(part)
    return jnp.concatenate(parts, axis=0)


def arrange_kernel(
    moves, far_rows, far_cols, far_order, down_tiles, up_tiles, held, weights, tile_rows, tile_cols, order, sems
):
    copies = [
        pltpu.make_async_copy(there, here, sems.at[k])
        for k, (there, here) in enumerate(
            ((far_rows, tile_rows), (far_cols, tile_cols), (far_order, order))
        )
    ]
    for copy in copies:
        copy.start()
    upward, _ = roles(moves)

    @pl.when(last_row())
    def _():
        weights[...] = held[...]

    @pl.when(jnp.logical_not(last_row()))
    def _():
        pl.when(upward)(lambda: transpose(up_tiles, weights))
        pl.when(jnp.logical_not(upward))(lambda: transpose(down_tiles, weights))

    for copy in copies:
        copy.wait()


def add_products(lists, group, pairs, columns, weights, total):
    column_bits, tile_bits = bits(weights.shape[0], total.shape[0])
    column_mask, tile_mask = 2**column_bits - 1, 2**tile_bits - 1
    for p in range(*pairs):
        word = lists[group * (lists.shape[0] // 3) + p, 0]
        one = word >> (column_bits + tile_bits)
        read = jnp.concatenate([columns[one & column_mask], columns[word & column_mask]], axis=1)
        tiles = (one >> column_bits) & tile_mask, (word >> column_bits) & tile_mask
        both = jnp.concatenate([weights[tiles[0]], weights[tiles[1]]], axis=0)
        row = one >> (column_bits + tile_bits)
        total[row] += jnp.dot(read, both, preferred_element_type=jnp.float32)


def stage_kernel(
    moves, final, group, lists, source, block, weights, before, down, up, other, trace, out, columns, total, *rest
):
    ready, sem = rest if group else (None, None)
    count, pairs = total.shape[0], lists.shape[0] // 3
    upward, _ = roles(moves)
    column_bits, tile_bits = bits(weights.shape[0], count)
    alone = no_farther(lax.axis_index("rows"), lax.axis_size("rows"))

    def place(k):
        return slice(k * TILE, (k + 1) * TILE)

    def ordered(value):
        return picked_rows(value.astype(jnp.float32), source[...]) if final else value

    def load():
        for k in range(count):
            read = block[0, :, place(k)]
            columns[k] = ordered(read).astype(columns.dtype) if group == 2 else read
            if before is None:
                total[k] = jnp.where(upward, up[0, :, place(k)], down[0, :, place(k)]).astype(jnp.float32)
            else:
                total[k] = before[k]
        columns[count] = jnp.zeros(columns.shape[1:], columns.dtype)

    def complete(value, other):
        for k in range(count):
            fresh = value[k].astype(jnp.bfloat16)
            if final:
                fresh = (fresh.astype(jnp.float32) + other[k]).astype(jnp.bfloat16)
            ready[0, :, place(k)] = fresh
        pltpu.make_async_copy(ready, trace, sem).start()

    def complete_wait():
        pltpu.make_async_copy(ready, trace, sem).wait()

    usual = -(-pairs // 2)

    def unusual(work):
        column = lists[group * pairs + usual, 0] >> (column_bits + tile_bits)

        @pl.when(column & (2**column_bits - 1) < count)
        def _():
            work()

    def add(low, high):
        add_products(lists, group, (low, high), columns, weights, total)

    if group == 0:
        load()
        add(0, pairs)
        out[...] = total[...]
    elif group == 1:
        load()
        add(0, usual)
        unusual(lambda: add(usual, pairs))
        for k in range(count):
            out[k] = ordered(total[k])
            if final:
                other[k] = ordered(jnp.where(upward, down[0, :, place(k)], up[0, :, place(k)]))

        @pl.when(alone)
        def _():
            complete(out, other)
            complete_wait()
    else:

        @pl.when(jnp.logical_not(alone))
        def _():
            load()
            add(0, usual)
            complete(total, other)

            def more():
                complete_wait()
                add(usual, pairs)
                complete(total, other)

            unusual(more)
            complete_wait()


def step(moves, final, down, up, down_tiles, up_tiles, tile_rows, tile_cols, order):
    rows = lax.axis_size("rows")
    _, shots, width = down.shape
    tiles, count = tile_rows.shape[1], width // TILE
    pairs = (tiles + min(tiles, count)) // 2
    shape = jax.ShapeDtypeStruct
    sums = shape((count, shots, TILE), jnp.float32)
    scratch = [pltpu.VMEM((count + 1, shots, TILE), jnp.bfloat16), pltpu.VMEM(sums.shape, sums.dtype)]

    leaving, _ = pick(moves, down, up, ())
    held, weights = hold(moves, leaving, down_tiles, up_tiles)
    first, distant = across(leaving, held, moves, rows)
    weights, *small = call(
        functools.partial(arrange_kernel, moves),
        "arrange",
        (shape((tiles, TILE, TILE), down_tiles.dtype), tile_rows, tile_cols, order),
        [pltpu.SemaphoreType.DMA((3,))],
        outside=3,
    )(tile_rows, tile_cols, order, down_tiles, up_tiles, weights)
    first, weights = lax.optimization_barrier((first, weights))
    second = lax.ppermute(first, "rows", [(r, partner(r, rows)) for r in range(rows)])

    def first_kernel(rows, cols, order, block, weights, down, up, out, lists, source, *scratch):
        list_pairs(moves, count, rows, cols, order, lists, source)
        stage_kernel(
            moves, final, 0, lists, source, block, weights, None, down, up, None, None, out, *scratch
        )

    def second_kernel(lists, source, block, weights, before, down, up, trace, out, other, *scratch):
        stage_kernel(
            moves, final, 1, lists, source, block, weights, before, down, up, other, trace, out, *scratch
        )

    def far_kernel(_, lists, source, block, weights, before, other, trace, *scratch):
        stage_kernel(
            moves, final, 2, lists, source, block, weights, before, None, None, other, trace, None, *scratch
        )

    total, lists, source = call(
        first_kernel,
        "first",
        (sums, shape((3 * pairs, TILE), jnp.int32), shape((shots, TILE), jnp.int32)),
        scratch,
        flops=3 * 10**9,
    )(*small, first, weights, down, up)
    scratch += [pltpu.VMEM(down.shape, down.dtype), pltpu.SemaphoreType.DMA]
    trace, total, other = call(second_kernel, "second", (down, sums, sums), scratch, outside_out=1)(
        lists, source, second, weights, total, down, up
    )
    (trace,) = call(far_kernel, "far", (down,), scratch, outside=1, outside_out=1, aliases={0: 0})(
        trace, lists, source, distant, weights, total, other
    )
    return trace


def shards(down_sources, up_sources, down_tiles, up_tiles, tile_rows, tile_cols, shot_order):
    order = shot_order.reshape(1, -1)
    steps = wavefront(lax.axis_size("layer"))
    down, up = down_sources, up_sources
    for at, moves in enumerate(steps):
        final = at == len(steps) - 1
        fresh = step(
            moves, final, down, up, down_tiles, up_tiles, tile_rows, tile_cols, order
        )
        if final:
            return fresh
        upward, _ = roles(moves)
        down, up = jnp.where(upward, down, fresh), jnp.where(upward, fresh, up)


def solution(mesh):
    return jax.shard_map(
        shards,
        mesh=mesh,
        in_specs=(
            P("layer", None, "rows"),
            P("layer", None, "rows"),
            P("layer", "rows", None, None),
            P("layer", "rows", None, None),
            P("layer", "rows"),
            P("layer", "rows"),
            P(),
        ),
        out_specs=P("layer", None, "rows"),
        check_vma=False,
    )
```

```python
import functools

import jax
import jax.numpy as jnp
from jax import lax
from jax.experimental import pallas as pl
from jax.experimental.pallas import tpu as pltpu
from jax.sharding import PartitionSpec as P

TILE = 128
VMEM_BYTES = 32 * 1024 * 1024


def wavefront(layers):
    steps = []
    for t in range(layers - 1):
        down, up = (t, t + 1), (layers - 1 - t, layers - 2 - t)
        if down[0] == up[0] or down[1] == up[1]:
            steps += [(down, None), (None, up)]
        else:
            steps.append((down, up))
    return steps


def partner(r, rows):
    other = r ^ 1
    return other if other < rows else r


def farther(r, rows):
    other = r + 1 if r % 2 else r - 1
    return other if 0 <= other < rows else r


def no_farther(r, rows):
    return (r == 0) | ((r == rows - 1) & (rows % 2 == 0))


def across(block, held, moves, rows):
    moves = [m for m in moves if m is not None]
    axes = ("layer", "rows")
    near = [(s * rows + r, d * rows + r) for s, d in moves for r in range(rows)]
    far = [(s * rows + r, d * rows + farther(r, rows)) for s, d in moves for r in range(rows)]
    return lax.ppermute(block, axes, near), lax.ppermute(held, axes, far)


def pick(moves, down, up, small):
    down_move, up_move = moves
    half = down.shape[1] // 2

    def kernel(down, up, *others):
        small, out, small_out, sems = others[:count], others[count], others[count + 1 : -1], others[-1]

        def copies(source):
            return [
                pltpu.make_async_copy(
                    source.at[:, pl.ds(k * half, half)], out.at[:, pl.ds(k * half, half)], sems.at[k]
                )
                for k in range(2)
            ]

        def start(source):
            for copy in copies(source):
                copy.start()

        if up_move is None:
            start(down)
        elif down_move is None:
            start(up)
        else:
            upward = lax.axis_index("layer") == up_move[0]
            pl.when(upward)(lambda: start(up))
            pl.when(jnp.logical_not(upward))(lambda: start(down))
        rest = [
            pltpu.make_async_copy(there, here, sems.at[2 + k])
            for k, (there, here) in enumerate(zip(small, small_out))
        ]
        for copy in rest:
            copy.start()
        for copy in copies(down) + rest:
            copy.wait()

    count = len(small)
    scratch = [pltpu.SemaphoreType.DMA((2 + count,))]
    leaving, *small = call(kernel, "pick", (down, *small), scratch, outside=2 + count)(down, up, *small)
    return leaving, small


def hold(moves, down_tiles, up_tiles, block):
    def kernel(down_tiles, up_tiles, block, weights, tiles, sem):
        @pl.when(last_row())
        def _():
            upward, _ = roles(moves)
            down_copy = pltpu.make_async_copy(down_tiles, tiles, sem)
            pl.when(upward)(lambda: pltpu.make_async_copy(up_tiles, tiles, sem).start())
            pl.when(jnp.logical_not(upward))(lambda: down_copy.start())
            down_copy.wait()
            transpose(tiles, weights)

    shape = jax.ShapeDtypeStruct
    return call(
        kernel,
        "hold",
        shape(down_tiles.shape[1:], down_tiles.dtype),
        [pltpu.VMEM(down_tiles.shape, down_tiles.dtype), pltpu.SemaphoreType.DMA],
        flops=3 * 10**9,
        outside=2,
    )(down_tiles, up_tiles, block)


def last_row():
    return lax.axis_index("rows") == lax.axis_size("rows") - 1


def transpose(tiles, weights):
    rows = lax.broadcasted_iota(jnp.int32, (TILE, TILE), 0)
    identity = (rows == lax.broadcasted_iota(jnp.int32, (TILE, TILE), 1)).astype(jnp.bfloat16)
    for t in range(weights.shape[0]):
        if t % 2:
            weights[t] = lax.dot_general(
                identity, tiles[0, t], (((1,), (1,)), ((), ())), preferred_element_type=jnp.float32
            ).astype(jnp.bfloat16)
        else:
            weights[t] = tiles[0, t].T


def call(kernel, name, out, scratch=(), flops=0, outside=0, outside_out=0, aliases={}):
    vmem = pl.BlockSpec(memory_space=pltpu.VMEM)
    shapes = jax.tree.map(lambda leaf: jax.ShapeDtypeStruct(leaf.shape, leaf.dtype), out)

    specs = jax.tree.map(lambda _: vmem, shapes)
    if outside_out:
        specs = tuple(pl.BlockSpec(memory_space=pl.ANY) if k < outside_out else vmem for k in range(len(shapes)))

    def run(*operands):
        operands = [
            pltpu.with_memory_space_constraint(operand, pltpu.HBM) if k < outside else operand
            for k, operand in enumerate(operands)
        ]
        return pl.pallas_call(
            kernel,
            out_shape=shapes,
            in_specs=[pl.BlockSpec(memory_space=pl.ANY)] * outside + [vmem] * (len(operands) - outside),
            out_specs=specs,
            scratch_shapes=scratch,
            input_output_aliases=aliases,
            compiler_params=pltpu.CompilerParams(vmem_limit_bytes=VMEM_BYTES),
            cost_estimate=pl.CostEstimate(flops=flops, bytes_accessed=0, transcendentals=0),
            name=name,
        )(*operands)

    return run


def roles(moves):
    layer = lax.axis_index("layer")
    down_move, up_move = moves
    upward = layer == (up_move[1] if up_move else -1)
    downward = layer == (down_move[1] if down_move else -1)
    return upward, jnp.logical_or(upward, downward)


def bits(tiles, count):
    return count.bit_length(), (tiles - 1).bit_length()


def list_pairs(moves, count, tile_rows, tile_cols, order, lists, source):
    _, active = roles(moves)
    me = lax.axis_index("rows")
    n, shots = tile_rows.shape[1], source.shape[0]
    pairs = lists.shape[0] // 3
    column_bits, tile_bits = bits(n, count)
    even = me % 2 == 0
    row = tile_rows[...] - me * count
    seen = tile_cols[...] - (me - 1) * count
    far_start = jnp.where(even, 0, 2 * count)
    far = (seen >= far_start) & (seen < far_start + count)
    own = (seen >= count) & (seen < 2 * count)
    group = jnp.where(far, 2, jnp.where(own, 0, 1))
    column = seen - jnp.where(seen < count, 0, jnp.where(seen < 2 * count, count, 2 * count))
    column = jnp.where(active, column, count)
    line = row + group * count
    line_l = jnp.broadcast_to(line.astype(jnp.float32), (n, n))
    both_s = (line_l * 2**column_bits + jnp.broadcast_to(column.astype(jnp.float32), (n, n))).T
    line_s = jnp.floor(both_s * 2.0**-column_bits)
    column_s = (both_s - line_s * 2**column_bits)[:, :1]
    t_l = lax.broadcasted_iota(jnp.int32, (n, n), 1)
    t_s = lax.broadcasted_iota(jnp.int32, (n, n), 0)
    same = line_l == line_s
    rank_l = jnp.sum(jnp.where(same & (t_s < t_l), 1.0, 0.0), axis=0, keepdims=True)
    rank_s = jnp.sum(jnp.where(same & (t_l < t_s), 1.0, 0.0), axis=1, keepdims=True)
    first_l = rank_l == 2.0 * jnp.floor(rank_l * 0.5)
    half_s = jnp.floor(rank_s * 0.5)
    first_s = rank_s == 2.0 * half_s
    group_s = jnp.where(line_s < count, 0.0, jnp.where(line_s < 2 * count, 1.0, 2.0))
    counted = (line_l < line_s) & (line_l >= group_s * count) & first_l
    ahead = jnp.sum(jnp.where(counted, 1.0, 0.0), axis=1, keepdims=True)
    slot = lax.broadcasted_iota(jnp.int32, (n, 3 * pairs), 1).astype(jnp.float32)
    hit = ahead + half_s + group_s[:, :1] * pairs == slot
    hit_a, hit_b = hit & first_s, hit & jnp.logical_not(first_s)

    def listed(hits, value):
        return jnp.sum(jnp.where(hits, value, 0.0), axis=0, keepdims=True)

    code_s = t_s[:, :1].astype(jnp.float32) * 2**column_bits + column_s - count
    row_s = (line_s - group_s * count)[:, :1] * 2 ** (column_bits + tile_bits)
    word = (listed(hit_a, row_s + code_s) + count) * 2 ** (column_bits + tile_bits)
    word = word + listed(hit_b, code_s) + count
    lists[...] = jnp.broadcast_to(word, (TILE, 3 * pairs)).T.astype(jnp.int32)

    wide = jnp.broadcast_to(order[...].astype(jnp.float32), (shots, shots))
    source[...] = jnp.broadcast_to(wide.T[:, :1], source.shape).astype(jnp.int32)


def picked_rows(value, source):
    groups = value.shape[0] // 8
    parts = []
    for i in range(groups):
        want = source[8 * i : 8 * i + 8]
        part = None
        for j in range(groups):
            found = jnp.take_along_axis(value[8 * j : 8 * j + 8], want & 7, axis=0)
            part = found if part is None else jnp.where(want >> 3 == j, found, part)
        parts.append(part)
    return jnp.concatenate(parts, axis=0)


def arrange_kernel(
    moves, far_rows, far_cols, far_order, down_tiles, up_tiles, held, weights, tile_rows, tile_cols, order, sems
):
    copies = [
        pltpu.make_async_copy(there, here, sems.at[k])
        for k, (there, here) in enumerate(
            ((far_rows, tile_rows), (far_cols, tile_cols), (far_order, order))
        )
    ]
    for copy in copies:
        copy.start()
    upward, _ = roles(moves)

    @pl.when(last_row())
    def _():
        weights[...] = held[...]

    @pl.when(jnp.logical_not(last_row()))
    def _():
        pl.when(upward)(lambda: transpose(up_tiles, weights))
        pl.when(jnp.logical_not(upward))(lambda: transpose(down_tiles, weights))

    for copy in copies:
        copy.wait()


def add_products(lists, group, pairs, columns, weights, total):
    column_bits, tile_bits = bits(weights.shape[0], total.shape[0])
    column_mask, tile_mask = 2**column_bits - 1, 2**tile_bits - 1
    for p in range(*pairs):
        word = lists[group * (lists.shape[0] // 3) + p, 0]
        one = word >> (column_bits + tile_bits)
        read = jnp.concatenate([columns[one & column_mask], columns[word & column_mask]], axis=1)
        tiles = (one >> column_bits) & tile_mask, (word >> column_bits) & tile_mask
        both = jnp.concatenate([weights[tiles[0]], weights[tiles[1]]], axis=0)
        row = one >> (column_bits + tile_bits)
        total[row] += jnp.dot(read, both, preferred_element_type=jnp.float32)


def stage_kernel(
    moves, final, group, lists, source, block, weights, before, down, up, other, trace, out, columns, total, *rest
):
    ready, sem = rest if group else (None, None)
    count, pairs = total.shape[0], lists.shape[0] // 3
    upward, _ = roles(moves)
    column_bits, tile_bits = bits(weights.shape[0], count)
    alone = no_farther(lax.axis_index("rows"), lax.axis_size("rows"))

    def place(k):
        return slice(k * TILE, (k + 1) * TILE)

    def ordered(value):
        return picked_rows(value.astype(jnp.float32), source[...]) if final else value

    def load():
        for k in range(count):
            read = block[0, :, place(k)]
            columns[k] = ordered(read).astype(columns.dtype) if group == 2 else read
            if before is None:
                total[k] = jnp.where(upward, up[0, :, place(k)], down[0, :, place(k)]).astype(jnp.float32)
            else:
                total[k] = before[k]
        columns[count] = jnp.zeros(columns.shape[1:], columns.dtype)

    def complete(value, other):
        for k in range(count):
            fresh = value[k].astype(jnp.bfloat16)
            if final:
                fresh = (fresh.astype(jnp.float32) + other[k]).astype(jnp.bfloat16)
            ready[0, :, place(k)] = fresh
        pltpu.make_async_copy(ready, trace, sem).start()

    def complete_wait():
        pltpu.make_async_copy(ready, trace, sem).wait()

    usual = -(-pairs // 2)

    def unusual(work):
        column = lists[group * pairs + usual, 0] >> (column_bits + tile_bits)

        @pl.when(column & (2**column_bits - 1) < count)
        def _():
            work()

    def add(low, high):
        add_products(lists, group, (low, high), columns, weights, total)

    if group == 0:
        load()
        add(0, pairs)
        out[...] = total[...]
    elif group == 1:
        load()
        add(0, usual)
        unusual(lambda: add(usual, pairs))
        for k in range(count):
            out[k] = ordered(total[k])
            if final:
                other[k] = ordered(jnp.where(upward, down[0, :, place(k)], up[0, :, place(k)]))

        @pl.when(alone)
        def _():
            complete(out, other)
            complete_wait()
    else:

        @pl.when(jnp.logical_not(alone))
        def _():
            load()
            add(0, usual)
            complete(total, other)

            def more():
                complete_wait()
                add(usual, pairs)
                complete(total, other)

            unusual(more)
            complete_wait()


def step(moves, final, down, up, down_tiles, up_tiles, tile_rows, tile_cols, order):
    rows = lax.axis_size("rows")
    _, shots, width = down.shape
    tiles, count = tile_rows.shape[1], width // TILE
    pairs = (tiles + min(tiles, count)) // 2
    shape = jax.ShapeDtypeStruct
    sums = shape((count, shots, TILE), jnp.float32)
    scratch = [pltpu.VMEM((count + 1, shots, TILE), jnp.bfloat16), pltpu.VMEM(sums.shape, sums.dtype)]

    leaving, _ = pick(moves, down, up, ())
    weights = hold(moves, down_tiles, up_tiles, leaving)
    held, weights = lax.optimization_barrier((leaving, weights))
    first, distant = across(leaving, held, moves, rows)
    weights, *small = call(
        functools.partial(arrange_kernel, moves),
        "arrange",
        (shape((tiles, TILE, TILE), down_tiles.dtype), tile_rows, tile_cols, order),
        [pltpu.SemaphoreType.DMA((3,))],
        outside=3,
    )(tile_rows, tile_cols, order, down_tiles, up_tiles, weights)
    first, weights = lax.optimization_barrier((first, weights))
    second = lax.ppermute(first, "rows", [(r, partner(r, rows)) for r in range(rows)])

    def first_kernel(rows, cols, order, block, weights, down, up, out, lists, source, *scratch):
        list_pairs(moves, count, rows, cols, order, lists, source)
        stage_kernel(
            moves, final, 0, lists, source, block, weights, None, down, up, None, None, out, *scratch
        )

    def second_kernel(lists, source, block, weights, before, down, up, trace, out, other, *scratch):
        stage_kernel(
            moves, final, 1, lists, source, block, weights, before, down, up, other, trace, out, *scratch
        )

    def far_kernel(_, lists, source, block, weights, before, other, trace, *scratch):
        stage_kernel(
            moves, final, 2, lists, source, block, weights, before, None, None, other, trace, None, *scratch
        )

    total, lists, source = call(
        first_kernel,
        "first",
        (sums, shape((3 * pairs, TILE), jnp.int32), shape((shots, TILE), jnp.int32)),
        scratch,
        flops=3 * 10**9,
    )(*small, first, weights, down, up)
    scratch += [pltpu.VMEM(down.shape, down.dtype), pltpu.SemaphoreType.DMA]
    trace, total, other = call(second_kernel, "second", (down, sums, sums), scratch, outside_out=1)(
        lists, source, second, weights, total, down, up
    )
    (trace,) = call(far_kernel, "far", (down,), scratch, outside=1, outside_out=1, aliases={0: 0})(
        trace, lists, source, distant, weights, total, other
    )
    return trace


def shards(down_sources, up_sources, down_tiles, up_tiles, tile_rows, tile_cols, shot_order):
    order = shot_order.reshape(1, -1)
    steps = wavefront(lax.axis_size("layer"))
    down, up = down_sources, up_sources
    for at, moves in enumerate(steps):
        final = at == len(steps) - 1
        fresh = step(
            moves, final, down, up, down_tiles, up_tiles, tile_rows, tile_cols, order
        )
        if final:
            return fresh
        upward, _ = roles(moves)
        down, up = jnp.where(upward, down, fresh), jnp.where(upward, fresh, up)


def solution(mesh):
    return jax.shard_map(
        shards,
        mesh=mesh,
        in_specs=(
            P("layer", None, "rows"),
            P("layer", None, "rows"),
            P("layer", "rows", None, None),
            P("layer", "rows", None, None),
            P("layer", "rows"),
            P("layer", "rows"),
            P(),
        ),
        out_specs=P("layer", None, "rows"),
        check_vma=False,
    )
```

```python
import functools

import jax
import jax.numpy as jnp
from jax import lax
from jax.experimental import pallas as pl
from jax.experimental.pallas import tpu as pltpu
from jax.sharding import PartitionSpec as P

TILE = 128
VMEM_BYTES = 32 * 1024 * 1024


def wavefront(layers):
    steps = []
    for t in range(layers - 1):
        down, up = (t, t + 1), (layers - 1 - t, layers - 2 - t)
        if down[0] == up[0] or down[1] == up[1]:
            steps += [(down, None), (None, up)]
        else:
            steps.append((down, up))
    return steps


def partner(r, rows):
    other = r ^ 1
    return other if other < rows else r


def farther(r, rows):
    other = r + 1 if r % 2 else r - 1
    return other if 0 <= other < rows else r


def no_farther(r, rows):
    return (r == 0) | ((r == rows - 1) & (rows % 2 == 0))


def across(block, held, moves, rows):
    moves = [m for m in moves if m is not None]
    axes = ("layer", "rows")
    near = [(s * rows + r, d * rows + r) for s, d in moves for r in range(rows)]
    far = [(s * rows + r, d * rows + farther(r, rows)) for s, d in moves for r in range(rows)]
    return lax.ppermute(block, axes, near), lax.ppermute(held, axes, far)


def pick(moves, down, up, small):
    down_move, up_move = moves
    half = down.shape[1] // 2

    def kernel(down, up, *others):
        small, out, small_out, sems = others[:count], others[count], others[count + 1 : -1], others[-1]

        def copies(source):
            return [
                pltpu.make_async_copy(
                    source.at[:, pl.ds(k * half, half)], out.at[:, pl.ds(k * half, half)], sems.at[k]
                )
                for k in range(2)
            ]

        def start(source):
            for copy in copies(source):
                copy.start()

        if up_move is None:
            start(down)
        elif down_move is None:
            start(up)
        else:
            upward = lax.axis_index("layer") == up_move[0]
            pl.when(upward)(lambda: start(up))
            pl.when(jnp.logical_not(upward))(lambda: start(down))
        rest = [
            pltpu.make_async_copy(there, here, sems.at[2 + k])
            for k, (there, here) in enumerate(zip(small, small_out))
        ]
        for copy in rest:
            copy.start()
        for copy in copies(down) + rest:
            copy.wait()

    count = len(small)
    scratch = [pltpu.SemaphoreType.DMA((2 + count,))]
    leaving, *small = call(kernel, "pick", (down, *small), scratch, outside=2 + count)(down, up, *small)
    return leaving, small


def hold(moves, down_tiles, up_tiles, block):
    def kernel(down_tiles, up_tiles, block, weights, tiles, sem):
        @pl.when(last_row())
        def _():
            upward, _ = roles(moves)
            down_copy = pltpu.make_async_copy(down_tiles, tiles, sem)
            pl.when(upward)(lambda: pltpu.make_async_copy(up_tiles, tiles, sem).start())
            pl.when(jnp.logical_not(upward))(lambda: down_copy.start())
            down_copy.wait()
            transpose(tiles, weights)

    shape = jax.ShapeDtypeStruct
    return call(
        kernel,
        "hold",
        shape(down_tiles.shape[1:], down_tiles.dtype),
        [pltpu.VMEM(down_tiles.shape, down_tiles.dtype), pltpu.SemaphoreType.DMA],
        flops=3 * 10**9,
        outside=2,
    )(down_tiles, up_tiles, block)


def last_row():
    return lax.axis_index("rows") == lax.axis_size("rows") - 1


def transpose(tiles, weights):
    rows = lax.broadcasted_iota(jnp.int32, (TILE, TILE), 0)
    identity = (rows == lax.broadcasted_iota(jnp.int32, (TILE, TILE), 1)).astype(jnp.bfloat16)
    for t in range(weights.shape[0]):
        if t % 2:
            weights[t] = lax.dot_general(
                identity, tiles[0, t], (((1,), (1,)), ((), ())), preferred_element_type=jnp.float32
            ).astype(jnp.bfloat16)
        else:
            weights[t] = tiles[0, t].T


def call(kernel, name, out, scratch=(), flops=0, outside=0, outside_out=0, aliases={}):
    vmem = pl.BlockSpec(memory_space=pltpu.VMEM)
    shapes = jax.tree.map(lambda leaf: jax.ShapeDtypeStruct(leaf.shape, leaf.dtype), out)

    specs = jax.tree.map(lambda _: vmem, shapes)
    if outside_out:
        specs = tuple(pl.BlockSpec(memory_space=pl.ANY) if k < outside_out else vmem for k in range(len(shapes)))

    def run(*operands):
        operands = [
            pltpu.with_memory_space_constraint(operand, pltpu.HBM) if k < outside else operand
            for k, operand in enumerate(operands)
        ]
        return pl.pallas_call(
            kernel,
            out_shape=shapes,
            in_specs=[pl.BlockSpec(memory_space=pl.ANY)] * outside + [vmem] * (len(operands) - outside),
            out_specs=specs,
            scratch_shapes=scratch,
            input_output_aliases=aliases,
            compiler_params=pltpu.CompilerParams(vmem_limit_bytes=VMEM_BYTES),
            cost_estimate=pl.CostEstimate(flops=flops, bytes_accessed=0, transcendentals=0),
            name=name,
        )(*operands)

    return run


def roles(moves):
    layer = lax.axis_index("layer")
    down_move, up_move = moves
    upward = layer == (up_move[1] if up_move else -1)
    downward = layer == (down_move[1] if down_move else -1)
    return upward, jnp.logical_or(upward, downward)


def bits(tiles, count):
    return count.bit_length(), (tiles - 1).bit_length()


def list_pairs(moves, count, tile_rows, tile_cols, order, lists, source):
    _, active = roles(moves)
    me = lax.axis_index("rows")
    n, shots = tile_rows.shape[1], source.shape[0]
    pairs = lists.shape[0] // 3
    column_bits, tile_bits = bits(n, count)
    even = me % 2 == 0
    row = tile_rows[...] - me * count
    seen = tile_cols[...] - (me - 1) * count
    far_start = jnp.where(even, 0, 2 * count)
    far = (seen >= far_start) & (seen < far_start + count)
    own = (seen >= count) & (seen < 2 * count)
    group = jnp.where(far, 2, jnp.where(own, 0, 1))
    column = seen - jnp.where(seen < count, 0, jnp.where(seen < 2 * count, count, 2 * count))
    column = jnp.where(active, column, count)
    line = row + group * count
    line_l = jnp.broadcast_to(line.astype(jnp.float32), (n, n))
    both_s = (line_l * 2**column_bits + jnp.broadcast_to(column.astype(jnp.float32), (n, n))).T
    line_s = jnp.floor(both_s * 2.0**-column_bits)
    column_s = (both_s - line_s * 2**column_bits)[:, :1]
    t_l = lax.broadcasted_iota(jnp.int32, (n, n), 1)
    t_s = lax.broadcasted_iota(jnp.int32, (n, n), 0)
    same = line_l == line_s
    rank_l = jnp.sum(jnp.where(same & (t_s < t_l), 1.0, 0.0), axis=0, keepdims=True)
    rank_s = jnp.sum(jnp.where(same & (t_l < t_s), 1.0, 0.0), axis=1, keepdims=True)
    first_l = rank_l == 2.0 * jnp.floor(rank_l * 0.5)
    half_s = jnp.floor(rank_s * 0.5)
    first_s = rank_s == 2.0 * half_s
    group_s = jnp.where(line_s < count, 0.0, jnp.where(line_s < 2 * count, 1.0, 2.0))
    counted = (line_l < line_s) & (line_l >= group_s * count) & first_l
    ahead = jnp.sum(jnp.where(counted, 1.0, 0.0), axis=1, keepdims=True)
    slot = lax.broadcasted_iota(jnp.int32, (n, 3 * pairs), 1).astype(jnp.float32)
    hit = ahead + half_s + group_s[:, :1] * pairs == slot
    hit_a, hit_b = hit & first_s, hit & jnp.logical_not(first_s)

    def listed(hits, value):
        return jnp.sum(jnp.where(hits, value, 0.0), axis=0, keepdims=True)

    code_s = t_s[:, :1].astype(jnp.float32) * 2**column_bits + column_s - count
    row_s = (line_s - group_s * count)[:, :1] * 2 ** (column_bits + tile_bits)
    word = (listed(hit_a, row_s + code_s) + count) * 2 ** (column_bits + tile_bits)
    word = word + listed(hit_b, code_s) + count
    lists[...] = jnp.broadcast_to(word, (TILE, 3 * pairs)).T.astype(jnp.int32)

    wide = jnp.broadcast_to(order[...].astype(jnp.float32), (shots, shots))
    source[...] = jnp.broadcast_to(wide.T[:, :1], source.shape).astype(jnp.int32)


def picked_rows(value, source):
    groups = value.shape[0] // 8
    parts = []
    for i in range(groups):
        want = source[8 * i : 8 * i + 8]
        part = None
        for j in range(groups):
            found = jnp.take_along_axis(value[8 * j : 8 * j + 8], want & 7, axis=0)
            part = found if part is None else jnp.where(want >> 3 == j, found, part)
        parts.append(part)
    return jnp.concatenate(parts, axis=0)


def arrange_kernel(
    moves, far_rows, far_cols, far_order, down_tiles, up_tiles, held, weights, tile_rows, tile_cols, order, sems
):
    copies = [
        pltpu.make_async_copy(there, here, sems.at[k])
        for k, (there, here) in enumerate(
            ((far_rows, tile_rows), (far_cols, tile_cols), (far_order, order))
        )
    ]
    for copy in copies:
        copy.start()
    upward, _ = roles(moves)

    @pl.when(last_row())
    def _():
        weights[...] = held[...]

    @pl.when(jnp.logical_not(last_row()))
    def _():
        pl.when(upward)(lambda: transpose(up_tiles, weights))
        pl.when(jnp.logical_not(upward))(lambda: transpose(down_tiles, weights))

    for copy in copies:
        copy.wait()


def add_products(lists, group, pairs, columns, weights, total):
    column_bits, tile_bits = bits(weights.shape[0], total.shape[0])
    column_mask, tile_mask = 2**column_bits - 1, 2**tile_bits - 1
    for p in range(*pairs):
        word = lists[group * (lists.shape[0] // 3) + p, 0]
        one = word >> (column_bits + tile_bits)
        read = jnp.concatenate([columns[one & column_mask], columns[word & column_mask]], axis=1)
        tiles = (one >> column_bits) & tile_mask, (word >> column_bits) & tile_mask
        both = jnp.concatenate([weights[tiles[0]], weights[tiles[1]]], axis=0)
        row = one >> (column_bits + tile_bits)
        total[row] += jnp.dot(read, both, preferred_element_type=jnp.float32)


def stage_kernel(
    moves, final, group, lists, source, block, weights, before, down, up, other, trace, out, columns, total, *rest
):
    ready, sem = rest if group else (None, None)
    count, pairs = total.shape[0], lists.shape[0] // 3
    upward, _ = roles(moves)
    column_bits, tile_bits = bits(weights.shape[0], count)
    alone = no_farther(lax.axis_index("rows"), lax.axis_size("rows"))

    def place(k):
        return slice(k * TILE, (k + 1) * TILE)

    def ordered(value):
        return picked_rows(value.astype(jnp.float32), source[...]) if final else value

    def load():
        for k in range(count):
            read = block[0, :, place(k)]
            columns[k] = ordered(read).astype(columns.dtype) if group == 2 else read
            if before is None:
                total[k] = jnp.where(upward, up[0, :, place(k)], down[0, :, place(k)]).astype(jnp.float32)
            else:
                total[k] = before[k]
        columns[count] = jnp.zeros(columns.shape[1:], columns.dtype)

    def complete(value, other):
        for k in range(count):
            fresh = value[k].astype(jnp.bfloat16)
            if final:
                fresh = (fresh.astype(jnp.float32) + other[k]).astype(jnp.bfloat16)
            ready[0, :, place(k)] = fresh
        pltpu.make_async_copy(ready, trace, sem).start()

    def complete_wait():
        pltpu.make_async_copy(ready, trace, sem).wait()

    usual = -(-pairs // 2) if group == 2 else -(-4 * pairs // 9)

    def unusual(work):
        column = lists[group * pairs + usual, 0] >> (column_bits + tile_bits)

        @pl.when(column & (2**column_bits - 1) < count)
        def _():
            work()

    def add(low, high):
        add_products(lists, group, (low, high), columns, weights, total)

    if group == 0:
        load()
        add(0, pairs)
        out[...] = total[...]
    elif group == 1:
        load()
        add(0, usual)
        unusual(lambda: add(usual, pairs))
        for k in range(count):
            out[k] = ordered(total[k])
            if final:
                other[k] = ordered(jnp.where(upward, down[0, :, place(k)], up[0, :, place(k)]))

        @pl.when(alone)
        def _():
            complete(out, other)
            complete_wait()
    else:

        @pl.when(jnp.logical_not(alone))
        def _():
            load()
            add(0, usual)
            complete(total, other)

            def more():
                complete_wait()
                add(usual, pairs)
                complete(total, other)

            unusual(more)
            complete_wait()


def step(moves, final, down, up, down_tiles, up_tiles, tile_rows, tile_cols, order):
    rows = lax.axis_size("rows")
    _, shots, width = down.shape
    tiles, count = tile_rows.shape[1], width // TILE
    pairs = (tiles + min(tiles, count)) // 2
    shape = jax.ShapeDtypeStruct
    sums = shape((count, shots, TILE), jnp.float32)
    scratch = [pltpu.VMEM((count + 1, shots, TILE), jnp.bfloat16), pltpu.VMEM(sums.shape, sums.dtype)]

    leaving, _ = pick(moves, down, up, ())
    weights = hold(moves, down_tiles, up_tiles, leaving)
    held, weights = lax.optimization_barrier((leaving, weights))
    first, distant = across(leaving, held, moves, rows)
    weights, *small = call(
        functools.partial(arrange_kernel, moves),
        "arrange",
        (shape((tiles, TILE, TILE), down_tiles.dtype), tile_rows, tile_cols, order),
        [pltpu.SemaphoreType.DMA((3,))],
        outside=3,
    )(tile_rows, tile_cols, order, down_tiles, up_tiles, weights)
    first, weights = lax.optimization_barrier((first, weights))
    second = lax.ppermute(first, "rows", [(r, partner(r, rows)) for r in range(rows)])

    def first_kernel(rows, cols, order, block, weights, down, up, out, lists, source, *scratch):
        list_pairs(moves, count, rows, cols, order, lists, source)
        stage_kernel(
            moves, final, 0, lists, source, block, weights, None, down, up, None, None, out, *scratch
        )

    def second_kernel(lists, source, block, weights, before, down, up, trace, out, other, *scratch):
        stage_kernel(
            moves, final, 1, lists, source, block, weights, before, down, up, other, trace, out, *scratch
        )

    def far_kernel(_, lists, source, block, weights, before, other, trace, *scratch):
        stage_kernel(
            moves, final, 2, lists, source, block, weights, before, None, None, other, trace, None, *scratch
        )

    total, lists, source = call(
        first_kernel,
        "first",
        (sums, shape((3 * pairs, TILE), jnp.int32), shape((shots, TILE), jnp.int32)),
        scratch,
        flops=3 * 10**9,
    )(*small, first, weights, down, up)
    scratch += [pltpu.VMEM(down.shape, down.dtype), pltpu.SemaphoreType.DMA]
    trace, total, other = call(second_kernel, "second", (down, sums, sums), scratch, outside_out=1)(
        lists, source, second, weights, total, down, up
    )
    (trace,) = call(far_kernel, "far", (down,), scratch, outside=1, outside_out=1, aliases={0: 0})(
        trace, lists, source, distant, weights, total, other
    )
    return trace


def shards(down_sources, up_sources, down_tiles, up_tiles, tile_rows, tile_cols, shot_order):
    order = shot_order.reshape(1, -1)
    steps = wavefront(lax.axis_size("layer"))
    down, up = down_sources, up_sources
    for at, moves in enumerate(steps):
        final = at == len(steps) - 1
        fresh = step(
            moves, final, down, up, down_tiles, up_tiles, tile_rows, tile_cols, order
        )
        if final:
            return fresh
        upward, _ = roles(moves)
        down, up = jnp.where(upward, down, fresh), jnp.where(upward, fresh, up)


def solution(mesh):
    return jax.shard_map(
        shards,
        mesh=mesh,
        in_specs=(
            P("layer", None, "rows"),
            P("layer", None, "rows"),
            P("layer", "rows", None, None),
            P("layer", "rows", None, None),
            P("layer", "rows"),
            P("layer", "rows"),
            P(),
        ),
        out_specs=P("layer", None, "rows"),
        check_vma=False,
    )
```
